512 devices in a mesh: dp: 16 (over y, core), proj: 32 (over x, z).
Axes of the slice: x: 4, y: 8, z: 8, core: 2. Of those that a mesh axis runs over, the one named last changes fastest.
Arguments:
- cotangents: bfloat16 [2048, 64, 8192], P(('dp', 'proj')), may hold values from -6 to 6
- adapter_activations: bfloat16 [2048, 64, 128], P(('dp', 'proj')), may hold values from -6 to 6
- lengths: int32 [2048], P(('dp', 'proj')), may hold values from 16 to 64
- column_factors: bfloat16 [4, 8192, 256], P(None, 'proj'), may hold values from -1 to 1, as said below
- row_factors: bfloat16 [4, 32, 32], replicated, may hold values from -1 to 1, as said below
- targets: bfloat16 [256, 8192], P('dp', 'proj'), may hold values from -16 to 16
Outputs:
- scores: float32 [2048, 256], P('dp')
The draws below stay inside these ranges and needn't reach their ends.
Inputs may be any that keep to these rules, and one draw needn't show every extreme that they name: `column_factors`: every entry is +1 or -1. `row_factors`: every entry is +1 or -1.
All inputs are finite; a program needn't handle non-finite values.
Results may differ from the reference program's by a relative error of at most 0.0029.
Values may be sent and summed in bfloat16 or wider, within the bound.
A program may use at most 128 MiB of HBM per device.

```python
import math
import jax
import jax.numpy as jnp
from jax import lax

MODEL_WIDTH = 8192
ADAPTER_RANK = 128
RG = 4
RS = 32
KR = 32
KC = 256
FEATURE_DIM = 8192
TOKEN_SLOTS = 64
E_DEV = 4
CANDIDATE_COUNT = 2048
NT = 256
N_PROJ = 32


def draw_lengths(key, part):
    key = jax.random.fold_in(key, 1)
    values = jax.random.randint(key, (CANDIDATE_COUNT,), TOKEN_SLOTS // 4, TOKEN_SLOTS + 1).astype(jnp.int32)
    return values.at[0].set(TOKEN_SLOTS).at[CANDIDATE_COUNT - 1].set(TOKEN_SLOTS // 4)


def draw_column_factors(key, part):
    key = jax.random.fold_in(key, 2)
    return jax.random.rademacher(key, (RG, MODEL_WIDTH, KC), jnp.float32).astype(jnp.bfloat16)


def draw_row_factors(key, part):
    key = jax.random.fold_in(key, 3)
    return jax.random.rademacher(key, (RG, RS, KR), jnp.float32).astype(jnp.bfloat16)


def draw_targets(key, part):
    key = jax.random.fold_in(key, 5)
    first = jax.random.fold_in(key, 0)
    rising = jnp.exp(jnp.log(3.0) * jnp.arange(FEATURE_DIM, dtype=jnp.float32) / FEATURE_DIM)
    values = jnp.clip(jax.random.normal(first, (NT, FEATURE_DIM), jnp.float32), -5.0, 5.0)
    return jnp.clip(values * rising, -16.0, 16.0).astype(jnp.bfloat16)


def block_scale(stream_key, extent, pieces, smallest, high):
    loudness, own = 1.0, jax.random.fold_in(stream_key, 6)
    for dim, shards_of in pieces:
        draws = jnp.exp(jax.random.uniform(jax.random.fold_in(own, dim), (shards_of,), jnp.float32, smallest / len(pieces), high / len(pieces)))
        loudness = loudness * jnp.repeat(draws, extent[dim] // shards_of).reshape([-1 if axis == dim else 1 for axis in range(len(extent))])
    return loudness


def normal_values(own_key, shape, spread, most, cuts=(), kind=jnp.bfloat16):
    level = block_scale(own_key, shape, cuts, -0.22, 0.18) if cuts else 1.0
    entries = jax.random.normal(own_key, shape, jnp.float32) * spread * level
    return jnp.minimum(jnp.maximum(entries, -most), most).astype(kind)


def setup_inputs(seed: int = 0) -> dict:
    arg_keys = jax.random.split(jax.random.key(seed), 7)
    cotangents = normal_values(arg_keys[0], (CANDIDATE_COUNT, TOKEN_SLOTS, MODEL_WIDTH), 1.0, 6.0, ((0, 512),))
    adapter_activations = normal_values(arg_keys[1], (CANDIDATE_COUNT, TOKEN_SLOTS, ADAPTER_RANK), 1.0, 6.0, ((0, 512),))
    lengths = draw_lengths(jax.random.fold_in(arg_keys[6], 71), 0)
    column_factors = draw_column_factors(jax.random.fold_in(arg_keys[6], 71), 0)
    row_factors = draw_row_factors(jax.random.fold_in(arg_keys[6], 71), 0)
    targets = draw_targets(jax.random.fold_in(arg_keys[6], 71), 0)
    return dict(cotangents=cotangents, adapter_activations=adapter_activations, lengths=lengths, column_factors=column_factors, row_factors=row_factors, targets=targets)


epsilon = 1e-06

def reference(cotangents, adapter_activations, lengths, column_factors, row_factors, targets):
    block_row_count = E_DEV * N_PROJ
    token_count = CANDIDATE_COUNT // block_row_count
    col_f32 = column_factors.astype(jnp.float32)
    row_f32 = row_factors.astype(jnp.float32)
    highest = lax.Precision.HIGHEST

    def compute_features(items):
        cot_block, act_block, len_block = items
        token_positions = lax.broadcasted_iota(jnp.int32, act_block.shape[:2], 1)
        token_valid_mask = (token_positions < len_block[:, None]).astype(jnp.float32)
        masked_values = act_block.astype(jnp.float32) * token_valid_mask[:, :, None]
        grads = jnp.einsum('etr,etd->erd', masked_values, cot_block.astype(jnp.float32), precision=highest)
        grads = grads.astype(jnp.bfloat16)
        split_rows = grads.astype(jnp.float32).reshape(block_row_count, RG, RS, MODEL_WIDTH)
        inner_terms = jnp.einsum('egad,gdc->egac', split_rows, col_f32, precision=highest)
        outer_terms = jnp.einsum('gak,egac->ekc', row_f32, inner_terms, precision=highest)
        return outer_terms.reshape(block_row_count, FEATURE_DIM)
    gradient_features = lax.map(compute_features, (cotangents.reshape(token_count, block_row_count, TOKEN_SLOTS, MODEL_WIDTH), adapter_activations.reshape(token_count, block_row_count, TOKEN_SLOTS, ADAPTER_RANK), lengths.reshape(token_count, block_row_count))).reshape(CANDIDATE_COUNT, FEATURE_DIM)
    target_f32 = targets.astype(jnp.float32)
    cand_sq = lax.optimization_barrier(jnp.sum(gradient_features * gradient_features, axis=1))
    targ_sq = lax.optimization_barrier(jnp.sum(target_f32 * target_f32, axis=1))
    dot_sums = jnp.dot(gradient_features, target_f32.T, precision=highest)
    return math.sqrt(FEATURE_DIM) * dot_sums / (jnp.sqrt(cand_sq + epsilon)[:, None] * jnp.sqrt(targ_sq + epsilon)[None, :])
```

```python
import functools
import math

import jax
import jax.numpy as jnp
from jax import lax
from jax.experimental import pallas as pl
from jax.experimental.pallas import tpu as pltpu
from jax.sharding import PartitionSpec as P

MESH = pl.DeviceIdType.MESH
EPS = 1e-06
XS, YS, ZS = 4, 8, 8
NP = XS * ZS
GR, RS, KR, KC = 4, 32, 32, 256
E, TOK, RANK = 4, 64, 128
HALF = 128
ROWS = (GR + 1) * HALF
ZX, ZX_GO, ZX_Y = 0, 256, 128
XZ, XZ_GO, XZ_Y = 384, 176, 80


def hop_order():
    offsets = [(dx, dz) for dx in (0, 1, -1, 2) for dz in (1, -1, 2, -2, 3, -3, 4, 0) if (dx, dz) != (0, 0)]
    return sorted(offsets, key=lambda o: (abs(o[0]) + abs(o[1]), abs(o[0])))


ORDER = hop_order()


def packed(i, values):
    words = [sum(v << (3 * k) for k, v in enumerate(values[w : w + 8])) for w in range(0, len(values), 8)]
    word = jnp.int32(words[0])
    for n, w in enumerate(words[1:], 1):
        word = jnp.where(i // 8 == n, jnp.int32(w), word)
    return (word >> (3 * (i % 8))) & 7


def kernel(
    cot_hbm, act_hbm, lens, cf_hbm, rf, tg_hbm, out,
    cot, act, masked, flipped, grads, big, acc, spread, part, part_in, tacc, halves, pay, land,
    lsem, ssem, msem, rzx, rxz, ryzx, ryxz,
):
    a, p = lax.axis_index("dp"), lax.axis_index("proj")
    y, c = a // 2, a % 2
    x, z = p // ZS, p % ZS
    odd = y % 2
    sib = (y * 2 + 1 - c, p)

    def at(ax, az):
        return (a, ((ax + XS) % XS) * ZS + (az + ZS) % ZS)

    def at_y(ay):
        return (((ay + YS) % YS) * 2 + c, p)

    bar = pltpu.get_barrier_semaphore()

    @pl.loop(1, NP)
    def _(i):
        pl.semaphore_signal(bar, inc=1, device_id=(a, (p + i) % NP), device_id_type=MESH)

    @pl.loop(1, 2 * YS)
    def _(i):
        pl.semaphore_signal(bar, inc=1, device_id=((a + i) % (2 * YS), p), device_id_type=MESH)

    own = []
    for g in range(GR):
        own.append(
            pltpu.make_async_copy(
                cf_hbm.at[g, pl.ds(pl.multiple_of(c * HALF, HALF), HALF)], big.at[p, pl.ds(g * HALF, HALF)], lsem.at[g]
            )
        )
    own_act = pltpu.make_async_copy(act_hbm, act, lsem.at[5])
    own_cot = pltpu.make_async_copy(cot_hbm, cot.at[pl.ds(c * E, E)], lsem.at[4])
    for copy in own:
        copy.start()
    own_act.start()
    own_cot.start()

    acc[...] = jnp.zeros_like(acc)
    tacc[...] = jnp.zeros_like(tacc)
    own_act.wait()
    tokens = lax.broadcasted_iota(jnp.int32, (TOK, RANK), 0)
    for e in range(E):
        kept = jnp.where(tokens < lens[e], act[e].astype(jnp.float32), 0.0)
        masked[c * E + e] = kept.astype(jnp.bfloat16)

    pl.semaphore_wait(bar, NP - 1 + 2 * YS - 1)

    def push(src, dst, s, r, to):
        pltpu.make_async_remote_copy(src_ref=src, dst_ref=dst, send_sem=s, recv_sem=r, device_id=to, device_id_type=MESH).start()

    def zx(j):
        return big.at[j, pl.ds(pl.multiple_of(ZX + ZX_Y * odd, 16), ZX_GO)]

    def xz(j):
        return big.at[j, pl.ds(pl.multiple_of(XZ + XZ_Y * odd, 16), XZ_GO)]

    def zx_y(j, plane):
        return big.at[j, pl.ds(pl.multiple_of(ZX + 256 * plane, 16), ZX_Y)]

    def xz_y(j, plane):
        return big.at[j, pl.ds(pl.multiple_of(XZ + 176 * plane, 16), XZ_Y)]

    def push_zx(j, to):
        push(zx(j), zx(j), ssem.at[0], rzx.at[j], to)

    def push_xz(j, to):
        push(xz(j), xz(j), ssem.at[1], rxz.at[j], to)

    def await_bytes(ref, sem):
        pltpu.make_async_copy(ref, ref, sem).wait()

    keeper = a // YS
    slot = big.at[p, pl.ds(pl.multiple_of(GR * HALF + 16 * (a % YS), 16), 16)]

    @pl.when(keeper == c)
    def _():
        pltpu.make_async_copy(tg_hbm, slot, msem.at[0]).start()

    @pl.when(keeper != c)
    def _():
        push(tg_hbm, slot, ssem.at[4], msem.at[0], sib)

    @pl.loop(1, YS)
    def _(i):
        push(tg_hbm, slot, ssem.at[4], msem.at[0], (((y + i) % YS) * 2 + keeper, p))

    for copy in own:
        copy.wait()
    for to in (at(x, z + 1), at(x, z - 1), at(x + 1, z), at(x - 1, z)):
        push_zx(p, to)

    mine, theirs = pl.ds(c * E, E), pl.ds((1 - c) * E, E)
    push(masked.at[mine], masked.at[mine], ssem.at[5], msem.at[1], sib)
    push(cot_hbm, cot.at[mine], ssem.at[6], msem.at[2], sib)

    await_bytes(big.at[p, pl.ds(GR * HALF, HALF)], msem.at[0])
    for to in (at(x + 1, z), at(x - 1, z), at(x, z + 1), at(x, z - 1)):
        push_xz(p, to)

    def candidate_grads(first):
        for e in range(E):
            flipped[first + e] = masked[first + e].astype(jnp.float32).T.astype(jnp.bfloat16)

        @pl.loop(0, E)
        def _(e):
            n = first + e
            left = flipped[n]
            row = pl.ds(pl.multiple_of(n * RS, RS), RS)

            @pl.loop(0, NP // 4)
            def _(q):
                for h in range(2):
                    pieces = [
                        cot[n, :, pl.ds(pl.multiple_of((4 * q + 2 * h + k) * 256 + c * HALF, HALF), HALF)] for k in range(2)
                    ]
                    right = jnp.concatenate(pieces, axis=1)
                    g_all = jnp.dot(left, right, preferred_element_type=jnp.float32).astype(jnp.bfloat16)
                    for g in range(GR):
                        grads[g, row, pl.ds(pl.multiple_of((4 * q + 2 * h) * HALF, 256), 256)] = g_all[g * RS : (g + 1) * RS]

    def block(j):
        columns = pl.ds(pl.multiple_of(j * HALF, HALF), HALF)
        for g in range(GR):
            acc[g] += jnp.dot(grads[g, :, columns], big[j, g * HALF : (g + 1) * HALF, :], preferred_element_type=jnp.float32)
        t = big[j, GR * HALF :, :].astype(jnp.float32)
        tacc[...] += t * t

    def offset(i):
        return packed(i, [o[0] + 1 for o in ORDER]) - 1, packed(i, [o[1] + 3 for o in ORDER]) - 3

    def source(i):
        dx, dz = offset(i)
        return dx, dz, (x - dx + XS) % XS, (z - dz + ZS) % ZS

    def hand_on(i):
        dx, dz, sx, sz = source(i)
        j = sx * ZS + sz
        step_z = jnp.where(dz > 0, 1, -1)
        far_z = jnp.abs(dz)
        to_y = 1 - 2 * ((sx + sz) % 2)

        await_bytes(zx(j), rzx.at[j])
        last_z = jnp.where(dz == 3, sz % 2 == 0, (dz == -3) & (sz % 2 == 1))

        @pl.when((dx == 0) & ((far_z < 3) | last_z))
        def _():
            push_zx(j, at(x, z + step_z))

        @pl.when(dx == 0)
        def _():
            push_zx(j, at(x + 1, z))
            push_zx(j, at(x - 1, z))

        @pl.when(((dx == 1) & (sz % 2 == 0)) | ((dx == -1) & (sz % 2 == 1)))
        def _():
            push_zx(j, at(x + dx, z))

        push(zx_y(j, odd), zx_y(j, odd), ssem.at[2], ryzx.at[j], at_y(y + to_y))

        await_bytes(xz(j), rxz.at[j])
        last_zx = jnp.where(dz == 3, sx % 2 == 0, (dz == -3) & (sx % 2 == 1))

        @pl.when((dz == 0) & (((dx == 1) & (sx % 2 == 0)) | ((dx == -1) & (sx % 2 == 1))))
        def _():
            push_xz(j, at(x + dx, z))

        @pl.when(dz == 0)
        def _():
            push_xz(j, at(x, z + 1))
            push_xz(j, at(x, z - 1))

        @pl.when((dz != 0) & ((far_z < 3) | last_zx))
        def _():
            push_xz(j, at(x, z + step_z))

        push(xz_y(j, odd), xz_y(j, odd), ssem.at[3], ryxz.at[j], at_y(y - to_y))

    def arrived_block(i):
        _, _, sx, sz = source(i)
        j = sx * ZS + sz
        await_bytes(zx_y(j, 1 - odd), ryzx.at[j])
        await_bytes(xz_y(j, 1 - odd), ryxz.at[j])
        block(j)

    own_cot.wait()
    candidate_grads(c * E)

    @pl.loop(0, 4)
    def _(i):
        hand_on(i)

    await_bytes(masked.at[theirs], msem.at[1])
    await_bytes(cot.at[theirs], msem.at[2])
    candidate_grads((1 - c) * E)
    block(p)

    big_rows = lax.broadcasted_iota(jnp.int32, (KR * 2 * E, KR), 0) // (2 * E)
    pick_k = (big_rows == lax.broadcasted_iota(jnp.int32, (KR * 2 * E, KR), 1)).astype(jnp.bfloat16)
    big_cols = lax.broadcasted_iota(jnp.int32, (RS, 2 * E * RS), 1) % RS
    pick_a = (big_cols == lax.broadcasted_iota(jnp.int32, (RS, 2 * E * RS), 0)).astype(jnp.bfloat16)
    same = lax.broadcasted_iota(jnp.int32, (256, 256), 0) % (2 * E) == lax.broadcasted_iota(jnp.int32, (256, 256), 1) // RS
    for g in range(GR):
        by_k = lax.dot_general(pick_k, rf[g], (((1,), (1,)), ((), ())), preferred_element_type=jnp.float32)
        wide = jnp.dot(by_k.astype(jnp.bfloat16), pick_a, preferred_element_type=jnp.float32)
        spread[g] = jnp.where(same, wide, 0.0).astype(jnp.bfloat16)

    def done_after(i):
        return jnp.maximum((i + 1) * 35 // 31 - 6, 0)

    @pl.loop(4, NP - 1)
    def _(i):
        hand_on(i)

        @pl.loop(done_after(i - 1), done_after(i))
        def _(k):
            arrived_block(k)

    @pl.loop(done_after(NP - 2), NP - 1)
    def _(k):
        arrived_block(k)

    total = jnp.zeros((KR * 2 * E, KC), jnp.float32)
    for g in range(GR):
        inner = acc[g]
        high = inner.astype(jnp.bfloat16)
        low = (inner - high.astype(jnp.float32)).astype(jnp.bfloat16)
        total += jnp.dot(spread[g], high, preferred_element_type=jnp.float32)
        total += jnp.dot(spread[g], low, preferred_element_type=jnp.float32)
    part[...] = total
    push(part, part_in, ssem.at[7], msem.at[3], sib)
    targ_sq = lax.dot_general(
        jnp.ones((2 * E, KC), jnp.float32), tacc[...], (((1,), (1,)), ((), ())),
        precision=lax.Precision.HIGHEST, preferred_element_type=jnp.float32,
    )
    await_bytes(part_in, msem.at[3])

    dots = jnp.zeros((4 * E, HALF), jnp.float32)
    squares = jnp.zeros((2 * E, KC), jnp.float32)
    for k in range(KR):
        feat = part[2 * E * k : 2 * E * (k + 1)] + part_in[2 * E * k : 2 * E * (k + 1)]
        squares += feat * feat
        high = feat.astype(jnp.bfloat16).astype(jnp.float32)
        both = jnp.concatenate([high, feat - high], axis=0).astype(jnp.bfloat16)
        dots += lax.dot_general(
            both, big[k, GR * HALF :, :], (((1,), (1,)), ((), ())), preferred_element_type=jnp.float32
        )
    cand_sq = jnp.sum(squares, axis=1, keepdims=True)
    product = dots[: 2 * E] + dots[2 * E :]
    scores = math.sqrt(KR * KC) * product / (jnp.sqrt(cand_sq + EPS) * jnp.sqrt(targ_sq + EPS))

    halves[c] = scores
    push(halves.at[c], halves.at[c], ssem.at[8], msem.at[4], sib)
    await_bytes(halves.at[1 - c], msem.at[4])
    for h in range(2):
        rows = halves[h]
        pay[E * h : E * (h + 1)] = jnp.where(c == 0, rows[:E], rows[E:])
    pltpu.make_async_copy(pay, land.at[p], msem.at[5]).start()

    @pl.loop(1, NP)
    def _(i):
        push(pay, land.at[p], ssem.at[9], msem.at[5], (a, (p + i) % NP))

    await_bytes(land, msem.at[5])
    for j in range(NP):
        for h in range(2):
            out[E * j : E * (j + 1), HALF * h : HALF * (h + 1)] = land[j, E * h : E * (h + 1)]

    rest = pl.ds(0, NP - 1)
    await_bytes(big.at[rest, pl.ds(0, ZX_GO)], ssem.at[0])
    await_bytes(big.at[rest, pl.ds(0, XZ_GO)], ssem.at[1])
    await_bytes(big.at[rest, pl.ds(0, ZX_Y)], ssem.at[2])
    await_bytes(big.at[rest, pl.ds(0, XZ_Y)], ssem.at[3])
    await_bytes(big.at[0, pl.ds(0, 16 * (YS - 1))], ssem.at[4])

    @pl.when(keeper != c)
    def _():
        await_bytes(big.at[0, pl.ds(0, 16)], ssem.at[4])

    await_bytes(masked.at[mine], ssem.at[5])
    await_bytes(cot.at[mine], ssem.at[6])
    await_bytes(part, ssem.at[7])
    await_bytes(halves.at[c], ssem.at[8])
    await_bytes(land.at[rest], ssem.at[9])


def on_device(cotangents, adapter_activations, lengths, column_factors, row_factors, targets):
    anywhere = pl.BlockSpec(memory_space=pl.ANY)
    vmem = pl.BlockSpec(memory_space=pltpu.VMEM)
    bf16, f32 = jnp.bfloat16, jnp.float32
    dma = pltpu.SemaphoreType.DMA
    return pl.pallas_call(
        kernel,
        out_shape=jax.ShapeDtypeStruct((NP * E, 2 * HALF), f32),
        in_specs=[anywhere, anywhere, pl.BlockSpec(memory_space=pltpu.SMEM), anywhere, vmem, anywhere],
        out_specs=vmem,
        scratch_shapes=[
            pltpu.VMEM((2 * E, TOK, NP * 256), bf16),
            pltpu.VMEM((E, TOK, RANK), bf16),
            pltpu.VMEM((2 * E, TOK, RANK), bf16),
            pltpu.VMEM((2 * E, RANK, TOK), bf16),
            pltpu.VMEM((GR, 2 * E * RS, NP * HALF), bf16),
            pltpu.VMEM((NP, ROWS, KC), bf16),
            pltpu.VMEM((GR, 2 * E * RS, KC), f32),
            pltpu.VMEM((GR, KR * 2 * E, 2 * E * RS), bf16),
            pltpu.VMEM((KR * 2 * E, KC), f32),
            pltpu.VMEM((KR * 2 * E, KC), f32),
            pltpu.VMEM((HALF, KC), f32),
            pltpu.VMEM((2, 2 * E, HALF), f32),
            pltpu.VMEM((2 * E, HALF), f32),
            pltpu.VMEM((NP, 2 * E, HALF), f32),
            dma((6,)),
            dma((10,)),
            dma((6,)),
            dma((NP,)),
            dma((NP,)),
            dma((NP,)),
            dma((NP,)),
        ],
        compiler_params=pltpu.CompilerParams(collective_id=0, has_side_effects=True, vmem_limit_bytes=56 * 2**20),
        cost_estimate=pl.CostEstimate(flops=3 * 10**9, bytes_accessed=6 * 2**20, transcendentals=0),
    )(cotangents, adapter_activations, lengths, column_factors, row_factors, targets)


def solution(mesh):
    placed = (
        P(("dp", "proj"), None, None),
        P(("dp", "proj"), None, None),
        P(("dp", "proj")),
        P(None, "proj", None),
        P(),
        P("dp", "proj"),
    )
    return jax.shard_map(on_device, mesh=mesh, in_specs=placed, out_specs=P("dp", None), check_vma=False)
```

```python
import functools
import math

import jax
import jax.numpy as jnp
from jax import lax
from jax.experimental import pallas as pl
from jax.experimental.pallas import tpu as pltpu
from jax.sharding import PartitionSpec as P

MESH = pl.DeviceIdType.MESH
EPS = 1e-06
XS, YS, ZS = 4, 8, 8
NP = XS * ZS
GR, RS, KR, KC = 4, 32, 32, 256
E, TOK, RANK = 4, 64, 128
HALF = 128
ROWS = (GR + 1) * HALF
ZX, ZX_GO, ZX_Y = 0, 256, 128
XZ, XZ_GO, XZ_Y = 384, 176, 80


OFFSETS = sorted(
    [(dx, dz) for dx in (0, 1, -1, 2) for dz in (1, -1, 2, -2, 3, -3, 4, 0)], key=lambda o: abs(o[0]) + abs(o[1])
)
SCHEDULE = [
    ("zx", 0, 0, "z+"), ("zx", 0, 0, "x-"), ("zx", 0, 0, "x+"), ("zx", 0, 0, "z-"), ("mine", 0, 0, ""),
    ("xz", 0, 0, "x+"), ("xz", 0, 0, "z+"), ("xz", 0, 0, "x-"), ("xz", 0, 0, "z-"), ("zx", 0, 1, "z+"),
    ("zx", 0, -1, "z-"), ("zx", 0, -1, "x+"), ("zx", 0, -1, "x-"), ("zx", 1, 0, "y"), ("zx", -1, 0, "y"),
    ("zx", 0, 1, "y"), ("xz", 1, 0, "x+"), ("xz", -1, 0, "y"), ("xz", 0, -1, "z-"), ("zx", 0, 1, "x+"),
    ("xz", 1, 0, "z+"), ("xz", -1, 0, "x-"), ("zx", 0, 1, "x-"), ("xz", 0, -1, "y"), ("zx", -1, 0, "x-"),
    ("xz", -1, 0, "z-"), ("xz", 0, 1, "z+"), ("xz", 0, 1, "y"), ("zx", 1, -1, "y"), ("zx", 1, -1, "x+"),
    ("zx", 0, 2, "z+"), ("zx", 0, 2, "y"), ("zx", 0, -2, "x-"), ("zx", 0, -2, "y"), ("zx", -1, -1, "x-"),
    ("zx", 0, -2, "z-"), ("zx", 0, -1, "y"), ("xz", 2, 0, "z+"), ("xz", 1, 0, "y"), ("zx", -1, -1, "y"),
    ("zx", 0, -2, "x+"), ("xz", 2, 0, "z-"), ("xz", 2, 0, "y"), ("xz", 0, -2, "y"), ("xz", 1, 1, "y"),
    ("xz", -1, 0, "z+"), ("xz", 1, 0, "z-"), ("zx", 1, 0, "x+"), ("xz", -1, -1, "y"), ("theirs", 0, 0, ""),
    ("zx", 0, 3, "y"), ("zx", -1, 1, "y"), ("zx", 0, -3, "z-"), ("zx", 0, 3, "x-"), ("zx", 0, 3, "z+"),
    ("xz", 0, 2, "y"), ("zx", 0, -3, "x+"), ("xz", 2, 1, "y"), ("zx", 0, -3, "y"), ("zx", 0, 2, "x-"),
    ("zx", 1, 1, "y"), ("zx", 0, 2, "x+"), ("xz", -1, -1, "z-"), ("zx", -1, 1, "x-"), ("zx", 2, -1, "y"),
    ("xz", -1, 1, "z+"), ("zx", -1, -2, "y"), ("zx", 2, 0, "y"), ("xz", 2, 1, "z+"), ("zx", -1, -2, "x-"),
    ("zx", 1, -2, "y"), ("zx", 0, -3, "x-"), ("xz", 2, -1, "y"), ("xz", 0, -2, "z-"), ("zx", 1, -2, "x+"),
    ("zx", 1, -3, "y"), ("xz", -1, 1, "y"), ("zx", 1, 1, "x+"), ("zx", 0, 4, "y"), ("xz", 1, -1, "z-"),
    ("xz", 1, 1, "z+"), ("zx", 0, 4, "x-"), ("xz", 2, -1, "z-"), ("xz", -1, 2, "z+"), ("xz", 1, -1, "y"),
    ("zx", -1, 3, "y"), ("xz", -1, 2, "y"), ("zx", 1, 2, "y"), ("xz", 0, 2, "z+"), ("xz", -1, -2, "z-"),
    ("zx", 0, 4, "x+"), ("zx", 0, 3, "x+"), ("xz", -1, -2, "y"), ("xz", 2, 2, "z+"), ("xz", 0, -3, "y"),
    ("zx", -1, 2, "y"), ("xz", 2, 2, "y"), ("group", 1, 0, ""), ("zx", 2, 1, "y"), ("xz", 1, 2, "y"),
    ("zx", -1, 2, "x-"), ("group", 2, 0, ""), ("zx", 2, -2, "y"), ("xz", 1, -2, "z-"), ("xz", 2, -2, "y"),
    ("xz", 1, 2, "z+"), ("xz", 2, -2, "z-"), ("zx", 1, 4, "y"), ("zx", -1, -3, "x-"), ("xz", -1, 3, "y"),
    ("zx", 1, -3, "x+"), ("zx", -1, -3, "y"), ("xz", -1, 3, "z+"), ("xz", -1, -3, "z-"), ("zx", 1, 2, "x+"),
    ("xz", 1, -2, "y"), ("zx", -1, 3, "x-"), ("xz", 0, -3, "z-"), ("zx", -1, 4, "y"), ("zx", 1, 4, "x+"),
    ("zx", 1, 3, "x+"), ("xz", 0, 3, "z+"), ("zx", 1, 3, "y"), ("xz", 2, 3, "z+"), ("zx", -1, 4, "x-"),
    ("xz", 1, -3, "y"), ("xz", 0, 3, "y"), ("xz", 2, 3, "y"), ("group", 0, 0, ""), ("xz", 1, 3, "y"),
    ("xz", 2, -3, "z-"), ("zx", 2, 2, "y"), ("xz", 1, 3, "z+"), ("xz", 2, -3, "y"), ("zx", 2, -3, "y"),
    ("xz", 1, -3, "z-"), ("xz", -1, 4, "y"), ("xz", 0, 4, "y"), ("zx", 2, 3, "y"), ("zx", 2, 4, "y"),
    ("group", 3, 0, ""), ("xz", 2, 4, "y"), ("group", 4, 0, ""), ("xz", 1, 4, "y"), ("xz", -1, -3, "y"),
    ("group", 5, 0, ""), ("group", 7, 0, ""), ("group", 6, 0, ""),
]
GROUP = 4


def kernel(
    cot_hbm, act_hbm, lens, cf_hbm, rf, tg_hbm, out,
    cot, act, masked, flipped, grads, big, tgt_in, acc, spread, part, part_in, tacc, tsq, tsq_in, pay, land,
    lsem, ssem, msem, rzx, rxz, ryzx, ryxz,
):
    a, p = lax.axis_index("dp"), lax.axis_index("proj")
    y, c = a // 2, a % 2
    x, z = p // ZS, p % ZS
    odd = y % 2
    sib = (y * 2 + 1 - c, p)

    def at(ax, az):
        return (a, ((ax + XS) % XS) * ZS + (az + ZS) % ZS)

    def at_y(ay):
        return (((ay + YS) % YS) * 2 + c, p)

    own = []
    for g in range(GR):
        own.append(
            pltpu.make_async_copy(
                cf_hbm.at[g, pl.ds(pl.multiple_of(c * HALF, HALF), HALF)], big.at[p, pl.ds(g * HALF, HALF)], lsem.at[g]
            )
        )
    own_act = pltpu.make_async_copy(act_hbm, act, lsem.at[5])
    own_cot = pltpu.make_async_copy(cot_hbm, cot.at[pl.ds(c * E, E)], lsem.at[4])
    for copy in own:
        copy.start()

    bar = pltpu.get_barrier_semaphore()

    @pl.loop(1, NP)
    def _(i):
        pl.semaphore_signal(bar, inc=1, device_id=(a, (p + i) % NP), device_id_type=MESH)

    @pl.loop(1, 2 * YS)
    def _(i):
        pl.semaphore_signal(bar, inc=1, device_id=((a + i) % (2 * YS), p), device_id_type=MESH)

    own_act.start()
    own_cot.start()
    for copy in own:
        copy.wait()
    pl.semaphore_wait(bar, NP - 1 + 2 * YS - 1)

    def push(src, dst, s, r, to):
        pltpu.make_async_remote_copy(src_ref=src, dst_ref=dst, send_sem=s, recv_sem=r, device_id=to, device_id_type=MESH).start()

    def zx(j):
        return big.at[j, pl.ds(pl.multiple_of(ZX + ZX_Y * odd, 16), ZX_GO)]

    def xz(j):
        return big.at[j, pl.ds(pl.multiple_of(XZ + XZ_Y * odd, 16), XZ_GO)]

    def zx_y(j, plane):
        return big.at[j, pl.ds(pl.multiple_of(ZX + ZX_GO * plane, 16), ZX_Y)]

    def xz_y(j, plane):
        return big.at[j, pl.ds(pl.multiple_of(XZ + XZ_GO * plane, 16), XZ_Y)]

    def push_zx(j, to):
        push(zx(j), zx(j), ssem.at[0], rzx.at[j], to)

    def push_xz(j, to):
        push(xz(j), xz(j), ssem.at[1], rxz.at[j], to)

    def await_bytes(ref, sem):
        pltpu.make_async_copy(ref, ref, sem).wait()

    keeper = a // YS
    slot = big.at[p, pl.ds(pl.multiple_of(GR * HALF + 16 * (a % YS), 16), 16)]

    @pl.when(keeper == c)
    def _():
        pltpu.make_async_copy(tg_hbm, slot, msem.at[0]).start()

    @pl.when(keeper != c)
    def _():
        push(tg_hbm, slot, ssem.at[4], msem.at[0], sib)

    @pl.loop(1, YS)
    def _(i):
        push(tg_hbm, slot, ssem.at[4], msem.at[0], (((y + i) % YS) * 2 + keeper, p))

    def candidate_grads(first):
        for e in range(E):
            flipped[first + e] = masked[first + e].astype(jnp.float32).T.astype(jnp.bfloat16)

        @pl.loop(0, E)
        def _(e):
            n = first + e
            row = pl.ds(pl.multiple_of(n * RS, RS), RS)
            for h in range(2):
                half = NP // 2
                pieces = [
                    cot[n, :, pl.ds(pl.multiple_of((h * half + k) * 256 + c * HALF, HALF), HALF)] for k in range(half)
                ]
                right = jnp.concatenate(pieces, axis=1)
                g_all = jnp.dot(flipped[n], right, preferred_element_type=jnp.float32).astype(jnp.bfloat16)
                for g in range(GR):
                    grads[g, row, h * half * HALF : (h + 1) * half * HALF] = g_all[g * RS : (g + 1) * RS]

    def source(dx, dz):
        sx, sz = (x - dx + XS) % XS, (z - dz + ZS) % ZS
        return sx, sz, sx * ZS + sz

    mine, theirs = pl.ds(c * E, E), pl.ds((1 - c) * E, E)

    def share_candidates():
        push(cot_hbm, cot.at[mine], ssem.at[6], msem.at[2], sib)
        own_act.wait()
        tokens = lax.broadcasted_iota(jnp.int32, (TOK, RANK), 0)
        for e in range(E):
            kept = jnp.where(tokens < lens[e], act[e].astype(jnp.float32), 0.0)
            masked[c * E + e] = kept.astype(jnp.bfloat16)
        push(masked.at[mine], masked.at[mine], ssem.at[5], msem.at[1], sib)

    held = set()

    def send(tree, dx, dz, way):
        sx, sz, j = source(dx, dz)
        if (tree, dx, dz) not in held:
            held.add((tree, dx, dz))
            if (dx, dz) != (0, 0):
                await_bytes(zx(j) if tree == "zx" else xz(j), (rzx if tree == "zx" else rxz).at[j])
            elif tree == "xz":
                await_bytes(big.at[p, pl.ds(GR * HALF, HALF)], msem.at[0])
        if way == "y":
            to_y = 1 - 2 * ((sx + sz) % 2)
            if tree == "zx":
                push(zx_y(j, odd), zx_y(j, odd), ssem.at[2], ryzx.at[j], at_y(y + to_y))
            else:
                push(xz_y(j, odd), xz_y(j, odd), ssem.at[3], ryxz.at[j], at_y(y - to_y))
            return
        step = 1 if way[1] == "+" else -1
        to = at(x + step, z) if way[0] == "x" else at(x, z + step)

        def go():
            (push_zx if tree == "zx" else push_xz)(j, to)

        if way[0] == "z" and abs(dz) == 3:
            pl.when((sz if tree == "zx" else sx) % 2 == (0 if dz > 0 else 1))(go)
        elif way[0] == "x" and abs(dx) == 1:
            pl.when((sz if tree == "zx" else sx) % 2 == (0 if dx > 0 else 1))(go)
        else:
            go()

    def multiply(offsets):
        js = [source(dx, dz)[2] for dx, dz in offsets]
        for (dx, dz), j in zip(offsets, js):
            if (dx, dz) != (0, 0):
                await_bytes(zx_y(j, 1 - odd), ryzx.at[j])
                await_bytes(xz_y(j, 1 - odd), ryxz.at[j])
            push(big.at[j, pl.ds(GR * HALF, HALF)], tgt_in.at[j], ssem.at[8], msem.at[4], sib)
        for g in range(GR):
            left = jnp.concatenate([grads[g, :, pl.ds(pl.multiple_of(j * HALF, HALF), HALF)] for j in js], axis=1)
            right = jnp.concatenate([big[j, g * HALF : (g + 1) * HALF, :] for j in js], axis=0)
            acc[g] += jnp.dot(left, right, preferred_element_type=jnp.float32)
        squares = tacc[...]
        for j in js:
            t = big[j, GR * HALF :, :].astype(jnp.float32)
            squares += t * t
        tacc[...] = squares

    def prepare():
        acc[...] = jnp.zeros_like(acc)
        tacc[...] = jnp.zeros_like(tacc)
        by_row = lax.broadcasted_iota(jnp.int32, (2 * KR * E, KR), 0) % (KR * E) // E
        pick_k = (by_row == lax.broadcasted_iota(jnp.int32, (2 * KR * E, KR), 1)).astype(jnp.bfloat16)
        by_col = lax.broadcasted_iota(jnp.int32, (RS, 2 * E * RS), 1) % RS
        pick_a = (by_col == lax.broadcasted_iota(jnp.int32, (RS, 2 * E * RS), 0)).astype(jnp.bfloat16)
        row = lax.broadcasted_iota(jnp.int32, (256, 256), 0)
        col = lax.broadcasted_iota(jnp.int32, (256, 256), 1) // RS
        same = row // (KR * E) * E + row % E == col
        for g in range(GR):
            by_k = lax.dot_general(pick_k, rf[g], (((1,), (1,)), ((), ())), preferred_element_type=jnp.float32)
            wide = jnp.dot(by_k.astype(jnp.bfloat16), pick_a, preferred_element_type=jnp.float32)
            spread[g] = jnp.where(same, wide, 0.0).astype(jnp.bfloat16)

    for n, (what, i, k, way) in enumerate(SCHEDULE):
        if what == "mine":
            own_cot.wait()
            candidate_grads(c * E)
        elif what == "theirs":
            await_bytes(masked.at[theirs], msem.at[1])
            await_bytes(cot.at[theirs], msem.at[2])
            candidate_grads((1 - c) * E)
            prepare()
        elif what == "group":
            multiply(OFFSETS[GROUP * i : GROUP * (i + 1)])
        else:
            send(what, i, k, way)
        if n == 3:
            share_candidates()

    total = jnp.zeros((2 * KR * E, KC), jnp.float32)
    for g in range(GR):
        inner = acc[g]
        high = inner.astype(jnp.bfloat16)
        low = (inner - high.astype(jnp.float32)).astype(jnp.bfloat16)
        total += jnp.dot(spread[g], high, preferred_element_type=jnp.float32)
        total += jnp.dot(spread[g], low, preferred_element_type=jnp.float32)
    part[...] = total.reshape(2, KR * E, KC)
    push(part.at[1 - c], part_in, ssem.at[7], msem.at[3], sib)
    tsq[...] = lax.dot_general(
        jnp.ones((2 * E, KC), jnp.float32), tacc[...], (((1,), (1,)), ((), ())),
        precision=lax.Precision.HIGHEST, preferred_element_type=jnp.float32,
    )
    push(tsq, tsq_in, ssem.at[10], msem.at[6], sib)
    await_bytes(tgt_in, msem.at[4])
    await_bytes(tsq_in, msem.at[6])
    await_bytes(part_in, msem.at[3])

    dots = [[jnp.zeros((4 * E, HALF), jnp.float32) for _ in range(2)] for _ in range(2)]
    squares = jnp.zeros((2 * E, KC), jnp.float32)
    for m in range(KR // 2):
        rows = slice(2 * E * m, 2 * E * (m + 1))
        feat = part[c, rows] + part_in[rows]
        squares += feat * feat
        high = feat.astype(jnp.bfloat16).astype(jnp.float32)
        both = jnp.concatenate([high, feat - high], axis=0).astype(jnp.bfloat16)
        for k in range(2):
            for h, t in enumerate((big[2 * m + k, GR * HALF :, :], tgt_in[2 * m + k])):
                dots[h][k] += lax.dot_general(both, t, (((1,), (1,)), ((), ())), preferred_element_type=jnp.float32)
    sums = jnp.sum(squares, axis=1, keepdims=True)
    cand_norm = jnp.sqrt(sums[:E] + sums[E:] + EPS)
    scores = []
    for h, t in enumerate((tsq, tsq_in)):
        even, late = dots[h]
        product = (even[:E] + even[2 * E : 3 * E]) + (late[E : 2 * E] + late[3 * E :])
        scores.append(math.sqrt(KR * KC) * product / (cand_norm * jnp.sqrt(t[:E] + EPS)))
    pay[:E] = jnp.where(c == 0, scores[0], scores[1])
    pay[E:] = jnp.where(c == 0, scores[1], scores[0])
    pltpu.make_async_copy(pay, land.at[p], msem.at[5]).start()

    @pl.loop(1, NP)
    def _(i):
        push(pay, land.at[p], ssem.at[9], msem.at[5], (a, (p + i) % NP))

    await_bytes(land, msem.at[5])
    for j in range(NP):
        for h in range(2):
            out[E * j : E * (j + 1), HALF * h : HALF * (h + 1)] = land[j, E * h : E * (h + 1)]

    rest = pl.ds(0, NP - 1)
    await_bytes(big.at[rest, pl.ds(0, ZX_GO)], ssem.at[0])
    await_bytes(big.at[rest, pl.ds(0, XZ_GO)], ssem.at[1])
    await_bytes(big.at[rest, pl.ds(0, ZX_Y)], ssem.at[2])
    await_bytes(big.at[rest, pl.ds(0, XZ_Y)], ssem.at[3])
    await_bytes(big.at[0, pl.ds(0, 16 * (YS - 1))], ssem.at[4])

    @pl.when(keeper != c)
    def _():
        await_bytes(big.at[0, pl.ds(0, 16)], ssem.at[4])

    await_bytes(masked.at[mine], ssem.at[5])
    await_bytes(cot.at[mine], ssem.at[6])
    await_bytes(part_in, ssem.at[7])
    await_bytes(tgt_in, ssem.at[8])
    await_bytes(land.at[rest], ssem.at[9])
    await_bytes(tsq, ssem.at[10])


def on_device(cotangents, adapter_activations, lengths, column_factors, row_factors, targets):
    anywhere = pl.BlockSpec(memory_space=pl.ANY)
    vmem = pl.BlockSpec(memory_space=pltpu.VMEM)
    bf16, f32 = jnp.bfloat16, jnp.float32
    dma = pltpu.SemaphoreType.DMA
    return pl.pallas_call(
        kernel,
        out_shape=jax.ShapeDtypeStruct((NP * E, 2 * HALF), f32),
        in_specs=[anywhere, anywhere, pl.BlockSpec(memory_space=pltpu.SMEM), anywhere, vmem, anywhere],
        out_specs=vmem,
        scratch_shapes=[
            pltpu.VMEM((2 * E, TOK, NP * 256), bf16),
            pltpu.VMEM((E, TOK, RANK), bf16),
            pltpu.VMEM((2 * E, TOK, RANK), bf16),
            pltpu.VMEM((2 * E, RANK, TOK), bf16),
            pltpu.VMEM((GR, 2 * E * RS, NP * HALF), bf16),
            pltpu.VMEM((NP, ROWS, KC), bf16),
            pltpu.VMEM((NP, HALF, KC), bf16),
            pltpu.VMEM((GR, 2 * E * RS, KC), f32),
            pltpu.VMEM((GR, KR * 2 * E, 2 * E * RS), bf16),
            pltpu.VMEM((2, KR * E, KC), f32),
            pltpu.VMEM((KR * E, KC), f32),
            pltpu.VMEM((HALF, KC), f32),
            pltpu.VMEM((2 * E, HALF), f32),
            pltpu.VMEM((2 * E, HALF), f32),
            pltpu.VMEM((2 * E, HALF), f32),
            pltpu.VMEM((NP, 2 * E, HALF), f32),
            dma((6,)),
            dma((11,)),
            dma((7,)),
            dma((NP,)),
            dma((NP,)),
            dma((NP,)),
            dma((NP,)),
        ],
        compiler_params=pltpu.CompilerParams(collective_id=0, has_side_effects=True, vmem_limit_bytes=56 * 2**20),
        cost_estimate=pl.CostEstimate(flops=3 * 10**9, bytes_accessed=6 * 2**20, transcendentals=0),
    )(cotangents, adapter_activations, lengths, column_factors, row_factors, targets)


def solution(mesh):
    placed = (
        P(("dp", "proj"), None, None),
        P(("dp", "proj"), None, None),
        P(("dp", "proj")),
        P(None, "proj", None),
        P(),
        P("dp", "proj"),
    )
    return jax.shard_map(on_device, mesh=mesh, in_specs=placed, out_specs=P("dp", None), check_vma=False)
```

```python
import functools
import math

import jax
import jax.numpy as jnp
from jax import lax
from jax.experimental import pallas as pl
from jax.experimental.pallas import tpu as pltpu
from jax.sharding import PartitionSpec as P

MESH = pl.DeviceIdType.MESH
EPS = 1e-06
XS, YS, ZS = 4, 8, 8
NP = XS * ZS
GR, RS, KR, KC = 4, 32, 32, 256
E, TOK, RANK = 4, 64, 128
HALF = 128
NB = NP // 2
ZX_ROWS = 336
XZ_ROWS = GR * HALF - ZX_ROWS
T_GO, T_Y = 80, 48


OFFSETS = sorted(
    [(dx, dz) for dx in (0, 1, -1, 2) for dz in (1, -1, 2, -2, 3, -3, 4, 0)], key=lambda o: abs(o[0]) + abs(o[1])
)
BY_PARITY = [[o for o in OFFSETS if sum(o) % 2 == parity] for parity in range(2)]
GROUP = 4
SCHEDULE = [
    (0, 0, 0, 0, "z-"), (1, 1, 0, 0, "x+"), (0, 0, 0, 0, "z+"), (1, 1, 0, 0, "x-"), (12, 0, 0, 0, ""), (2, 0, 0, 0, "z+"),
    (2, 0, 0, 0, "x-"), (2, 0, 0, 0, "z-"), (2, 0, 0, 0, "x+"), (2, 1, 0, 0, "x+"), (1, 1, -1, 0, "x-"), (1, 1, -1, 0, "z-"),
    (1, 1, 0, 0, "z-"), (1, 1, -1, 0, "z+"), (1, 1, 0, 0, "z+"), (1, 1, 1, 0, "x+"), (0, 0, 0, 0, "x-"), (2, 1, 0, 0, "z-"),
    (2, 1, 0, 0, "z+"), (2, 0, 0, 1, "z+"), (2, 0, 0, -1, "x+"), (2, 0, 0, 1, "x+"), (0, 0, 0, 1, "x+"), (2, 0, 0, -1, "x-"),
    (0, 0, 0, -1, "z-"), (0, 0, 0, -1, "x-"), (0, 0, 0, -1, "x+"), (0, 0, 0, 0, "x+"), (0, 0, 0, 1, "z+"), (2, 0, 0, -1, "z-"),
    (2, 0, 0, 2, "z+"), (2, 1, 0, 0, "x-"), (0, 0, 0, 1, "x-"), (2, 1, 0, 1, "z+"), (2, 1, 1, 0, "x+"), (2, 1, 1, 0, "z+"),
    (2, 1, 1, 0, "z-"), (1, 1, 2, 0, "z-"), (2, 0, 0, -2, "z-"), (2, 0, 0, 1, "x-"), (1, 1, 2, 0, "z+"), (0, 0, 0, 2, "x-"),
    (0, 0, 0, 2, "z+"), (0, 0, 0, -2, "z-"), (0, 0, 0, 2, "x+"), (2, 1, -1, 0, "z-"), (2, 0, 0, -3, "z-"), (2, 0, 0, 2, "x-"),
    (2, 0, 0, 2, "x+"), (0, 0, 0, -2, "x-"), (2, 1, -1, 0, "x-"), (2, 0, 0, 3, "x-"), (2, 0, 1, 1, "x+"), (2, 0, 0, 3, "x+"),
    (0, 0, 0, -2, "x+"), (2, 1, -1, 0, "z+"), (2, 0, 0, -2, "x+"), (1, 1, 0, -1, "z-"), (2, 1, 1, -1, "z-"), (1, 1, 1, 0, "z-"),
    (2, 0, -1, -1, "x-"), (2, 0, 0, -3, "x-"), (2, 0, 0, -2, "x-"), (1, 1, 0, 1, "z+"), (0, 0, 1, 0, "x+"), (2, 0, 1, -1, "x+"),
    (1, 1, -1, 1, "z+"), (2, 1, -1, -1, "z-"), (2, 0, -1, 2, "x-"), (2, 0, 1, 2, "x+"), (1, 1, -1, -1, "z-"), (1, 1, 1, 0, "z+"),
    (2, 0, 0, 3, "z+"), (2, 0, -1, 1, "x-"), (1, 1, 2, 1, "z+"), (2, 1, -1, 1, "z+"), (2, 1, 2, 0, "z-"), (2, 0, 0, -3, "x+"),
    (2, 1, 2, 0, "z+"), (1, 1, 2, -1, "z-"), (0, 0, 0, 3, "z+"), (0, 0, 0, -3, "x-"), (0, 0, 0, -3, "x+"), (0, 0, 1, 1, "x+"),
    (0, 0, 0, -3, "z-"), (0, 0, 0, 3, "x-"), (0, 0, -1, 0, "x-"), (2, 0, -1, 1, "y"), (12, 1, 0, 0, ""), (1, 1, 1, -1, "z-"),
    (1, 1, 1, 1, "z+"), (2, 0, -1, -2, "y"), (2, 0, 0, -1, "y"), (0, 0, 1, -1, "x+"), (2, 1, 1, -2, "z-"), (2, 0, 1, -2, "x+"),
    (0, 0, 0, 3, "x+"), (2, 1, 1, 1, "z+"), (2, 1, 2, 1, "z+"), (2, 1, 0, -1, "z-"), (2, 0, 1, -1, "y"), (2, 0, 0, 4, "x+"),
    (1, 1, -1, 2, "z+"), (2, 1, -1, -2, "z-"), (0, 0, -1, 1, "x-"), (2, 1, 2, -1, "z-"), (1, 1, 0, 2, "z+"), (0, 0, 1, -2, "x+"),
    (0, 0, -1, 2, "x-"), (1, 1, 0, -2, "z-"), (2, 0, -1, 2, "y"), (2, 1, 0, 2, "z+"), (2, 1, -1, 2, "z+"), (0, 0, -1, -1, "x-"),
    (0, 0, 0, 4, "x+"), (0, 0, 0, 4, "x-"), (2, 0, 1, -3, "x+"), (2, 1, 1, -3, "z-"), (2, 0, 2, 1, "y"), (2, 0, 1, 3, "x+"),
    (2, 0, -1, 0, "x-"), (2, 0, -1, -3, "x-"), (2, 0, -1, 3, "x-"), (1, 1, -1, -2, "z-"), (2, 0, 1, -3, "y"), (1, 1, 1, -2, "z-"),
    (1, 1, 2, 2, "z+"), (2, 1, 1, 2, "z+"), (2, 1, 0, -2, "z-"), (2, 0, 1, 0, "y"), (2, 0, 1, 0, "x+"), (1, 1, 2, -2, "z-"),
    (2, 0, 0, 4, "x-"), (1, 1, 1, 2, "z+"), (12, 2, 0, 0, ""), (2, 0, -1, -3, "y"), (2, 0, 2, 2, "y"), (2, 1, 2, -2, "z-"),
    (2, 1, -1, -3, "z-"), (2, 0, -1, -2, "x-"), (0, 0, -1, 3, "x-"), (2, 0, 2, -1, "y"), (0, 0, 1, -3, "x+"), (2, 1, 1, 3, "z+"),
    (1, 1, 0, 3, "z+"), (2, 0, -1, 3, "y"), (2, 1, -1, 3, "z+"), (0, 0, 1, 2, "x+"), (0, 0, -1, -2, "x-"), (1, 1, 0, -3, "z-"),
    (0, 0, 1, 4, "x+"), (0, 0, -1, -3, "x-"), (2, 1, 2, 2, "z+"), (1, 1, -1, -3, "z-"), (1, 1, -1, 3, "z+"), (1, 1, 2, 3, "z+"),
    (2, 0, 0, 1, "y"), (0, 0, 1, 3, "x+"), (2, 1, 0, 3, "z+"), (2, 1, 0, -3, "z-"), (0, 0, -1, 4, "x-"), (2, 0, 1, 1, "y"),
    (14, 0, 0, 0, ""), (1, 1, 1, -3, "z-"), (1, 1, 1, 3, "z+"), (13, 1, 0, 0, ""), (2, 0, 0, 2, "y"), (2, 0, 1, -2, "y"),
    (1, 1, 2, -3, "z-"), (2, 0, 0, 3, "y"), (2, 0, -1, 4, "x-"), (13, 0, 0, 0, ""), (2, 0, -1, -1, "y"), (2, 0, 1, 4, "x+"),
    (2, 0, 2, -3, "y"), (2, 0, 2, 3, "y"), (14, 1, 0, 0, ""), (2, 1, 2, -3, "z-"), (2, 0, 0, -3, "y"), (2, 0, 0, -2, "y"),
    (2, 0, 1, 4, "y"), (2, 1, 2, 3, "z+"), (2, 0, -1, 4, "y"), (14, 2, 0, 0, ""), (2, 0, 2, -2, "y"), (2, 0, 1, 3, "y"),
    (13, 2, 0, 0, ""), (2, 0, 0, 4, "y"), (2, 0, 2, 0, "y"), (2, 0, -1, 0, "y"), (2, 0, 1, 2, "y"), (13, 3, 0, 0, ""),
    (14, 3, 0, 0, ""), (2, 0, 2, 4, "y"), (16, 0, 0, 0, ""), (15, 2, 0, 0, ""), (15, 3, 0, 0, ""), (15, 0, 0, 0, ""),
    (15, 1, 0, 0, ""),
]


def kernel(
    cot_hbm, act_hbm, lens, cf_hbm, rf, tg_hbm, out,
    cot, act, masked, flipped, grads, big, tgt, tgt_in, acc, spread, part, part_in, tacc, tsq, tsq_in, pay, land,
    lsem, ssem, msem, csem, rzx, rxz, rt, rty,
):
    a, p = lax.axis_index("dp"), lax.axis_index("proj")
    y, c = a // 2, a % 2
    x, z = p // ZS, p % ZS
    odd = y % 2
    outside = (x + z + odd) % 2
    sib = (y * 2 + 1 - c, p)

    def at(ax, az):
        return (a, ((ax + XS) % XS) * ZS + (az + ZS) % ZS)

    def at_y(ay, core):
        return (((ay + YS) % YS) * 2 + core, p)

    def partner_y(core):
        return y + (1 - 2 * odd) * (1 - 2 * core)

    def push(src, dst, s, r, to):
        pltpu.make_async_remote_copy(src_ref=src, dst_ref=dst, send_sem=s, recv_sem=r, device_id=to, device_id_type=MESH).start()

    def await_bytes(ref, sem):
        pltpu.make_async_copy(ref, ref, sem).wait()

    def cot_columns(q, parity, half):
        sx = q // 4
        j = sx * ZS + 2 * (q % 4) + (sx + parity) % 2
        return cot_hbm.at[:, :, pl.ds(pl.multiple_of(j * 256 + half * HALF, HALF), HALF)]

    def cot_slot(who, q):
        return cot.at[who, :, :, pl.ds(pl.multiple_of(q * HALF, HALF), HALF)]

    own = []
    for g in range(GR):
        own.append(
            pltpu.make_async_copy(
                cf_hbm.at[g, pl.ds(pl.multiple_of(c * HALF, HALF), HALF)], big.at[p // 2, pl.ds(g * HALF, HALF)], lsem.at[g]
            )
        )
    own_act = pltpu.make_async_copy(act_hbm, act, lsem.at[5])

    @pl.when(outside == 0)
    def _():
        for copy in own:
            copy.start()

    bar = pltpu.get_barrier_semaphore()

    @pl.loop(1, NP)
    def _(i):
        pl.semaphore_signal(bar, inc=1, device_id=(a, (p + i) % NP), device_id_type=MESH)

    @pl.loop(1, 2 * YS)
    def _(i):
        pl.semaphore_signal(bar, inc=1, device_id=((a + i) % (2 * YS), p), device_id_type=MESH)

    own_act.start()

    @pl.loop(0, NB)
    def _(q):
        pltpu.make_async_copy(cot_columns(q, odd, c), cot_slot(c, q), lsem.at[4]).start()

    @pl.when(outside == 0)
    def _():
        for copy in own:
            copy.wait()

    pl.semaphore_wait(bar, NP - 1 + 2 * YS - 1)

    keeper = a // YS
    slot = tgt.at[p, pl.ds(pl.multiple_of(16 * (a % YS), 16), 16)]

    @pl.when(keeper == c)
    def _():
        pltpu.make_async_copy(tg_hbm, slot, msem.at[0]).start()

    @pl.when(keeper != c)
    def _():
        push(tg_hbm, slot, ssem.at[4], msem.at[0], sib)

    @pl.loop(1, YS)
    def _(i):
        push(tg_hbm, slot, ssem.at[4], msem.at[0], at_y(y + i, keeper))

    def zx(j):
        return big.at[j // 2, pl.ds(0, ZX_ROWS)]

    def xz(j):
        return big.at[j // 2, pl.ds(ZX_ROWS, XZ_ROWS)]

    def t_go(j):
        return tgt.at[j, pl.ds(pl.multiple_of(T_Y * odd, 16), T_GO)]

    def t_y(j, plane):
        return tgt.at[j, pl.ds(pl.multiple_of(T_GO * plane, 16), T_Y)]

    PARTS = ((zx, rzx), (xz, rxz), (t_go, rt))

    def source(dx, dz):
        sx, sz = (x - dx + XS) % XS, (z - dz + ZS) % ZS
        return sx, sz, sx * ZS + sz

    def share_candidates():
        own_act.wait()
        tokens = lax.broadcasted_iota(jnp.int32, (TOK, RANK), 0)
        for e in range(E):
            kept = jnp.where(tokens < lens[e], act[e].astype(jnp.float32), 0.0)
            masked[c, e] = kept.astype(jnp.bfloat16)
        for h in range(2):
            push(masked.at[c], masked.at[2 + c], ssem.at[5], msem.at[1 + c], at_y(partner_y(h), h))

        @pl.loop(0, NB)
        def _(q):
            for h in range(2):
                push(cot_columns(q, 1 - odd, h), cot_slot(2 + c, q), ssem.at[6], csem.at[2 + c], at_y(partner_y(h), h))

        push(masked.at[c], masked.at[c], ssem.at[5], msem.at[7], sib)

        @pl.loop(0, NB)
        def _(q):
            push(cot_columns(q, odd, 1 - c), cot_slot(c, q), ssem.at[6], csem.at[0], sib)

    def candidate_grads(who):
        for e in range(E):
            flipped[who, e] = masked[who, e].astype(jnp.float32).T.astype(jnp.bfloat16)

        @pl.loop(0, E)
        def _(e):
            row = pl.ds(pl.multiple_of((who * E + e) * RS, RS), RS)
            g_all = jnp.dot(flipped[who, e], cot[who, e], preferred_element_type=jnp.float32).astype(jnp.bfloat16)
            for g in range(GR):
                grads[g, row, :] = g_all[g * RS : (g + 1) * RS]

    def prepare():
        acc[...] = jnp.zeros_like(acc)
        tacc[...] = jnp.zeros_like(tacc)
        by_row = lax.broadcasted_iota(jnp.int32, (2 * KR * E, KR), 0) % (KR * E) // E
        pick_k = (by_row == lax.broadcasted_iota(jnp.int32, (2 * KR * E, KR), 1)).astype(jnp.bfloat16)
        by_col = lax.broadcasted_iota(jnp.int32, (RS, 2 * E * RS), 1) % RS
        pick_a = (by_col == lax.broadcasted_iota(jnp.int32, (RS, 2 * E * RS), 0)).astype(jnp.bfloat16)
        row = lax.broadcasted_iota(jnp.int32, (256, 256), 0)
        col = lax.broadcasted_iota(jnp.int32, (256, 256), 1) // RS
        same = row // (KR * E) * E + row % E == col
        for g in range(GR):
            by_k = lax.dot_general(pick_k, rf[g], (((1,), (1,)), ((), ())), preferred_element_type=jnp.float32)
            wide = jnp.dot(by_k.astype(jnp.bfloat16), pick_a, preferred_element_type=jnp.float32)
            spread[g] = jnp.where(same, wide, 0.0).astype(jnp.bfloat16)

    held = set()
    sent = [jnp.int32(0)] * 3

    def await_part(stream, dx, dz, parities):
        new = [r for r in parities if (stream, dx, dz, r) not in held]
        held.update((stream, dx, dz, r) for r in new)
        if not new or (dx, dz) == (0, 0) and stream < 2:
            return
        view, sems = PARTS[stream]
        j = source(dx, dz)[2]

        def go():
            if (dx, dz) == (0, 0):
                await_bytes(tgt.at[p], msem.at[0])
            else:
                await_bytes(view(j), sems.at[j])

        if len(new) == 2:
            go()
        else:
            pl.when((dx + dz + outside) % 2 == new[0])(go)

    def send(stream, tree, dx, dz, way):
        sx, sz, j = source(dx, dz)
        view, sems = PARTS[stream]
        if way == "y":
            await_part(stream, dx, dz, (0, 1))
            to_y = 1 - 2 * ((sx + sz // 2) % 2)
            push(t_y(j, odd), t_y(j, odd), ssem.at[3], rty.at[j], at_y(y + to_y, c))
            return
        parity = 0 if stream < 2 else 1 - tree
        await_part(stream, dx, dz, (parity,))
        step = 1 if way[1] == "+" else -1
        to = at(x + step, z) if way[0] == "x" else at(x, z + step)
        applies = (dx + dz + outside) % 2 == parity
        side = (sz if tree == 0 else sx) // 2 % 2
        if way[0] == "z" and abs(dz) == 3:
            applies &= side == (0 if dz > 0 else 1)
        elif way[0] == "x" and abs(dx) == 1:
            applies &= side == (0 if dx > 0 else 1)
        sent[stream] += applies.astype(jnp.int32)

        @pl.when(applies)
        def _():
            push(view(j), view(j), ssem.at[stream], sems.at[j], to)

    def multiply(q, side):
        members = [[offsets[GROUP * q + i] for offsets in BY_PARITY] for i in range(GROUP)]
        for pair in members:
            for o in pair:
                for stream in range(2):
                    await_part(stream, *o, (0,))
        js = [jnp.where(outside == 0, source(*even)[2], source(*odds)[2]) // 2 for even, odds in members]
        rows = slice(256 * side, 256 * (side + 1))
        for g in range(GR):
            left = jnp.concatenate([grads[g, rows, pl.ds(pl.multiple_of(j * HALF, HALF), HALF)] for j in js], axis=1)
            right = jnp.concatenate([big[j, g * HALF : (g + 1) * HALF, :] for j in js], axis=0)
            acc[g, side] += jnp.dot(left, right, preferred_element_type=jnp.float32)

    def targets_done(q):
        squares = tacc[...]
        for dx, dz in OFFSETS[8 * q : 8 * (q + 1)]:
            j = source(dx, dz)[2]
            await_part(2, dx, dz, (0, 1))
            if (dx, dz) != (0, 0):
                await_bytes(t_y(j, 1 - odd), rty.at[j])
            push(tgt.at[j], tgt_in.at[j], ssem.at[8], msem.at[4], sib)
            t = tgt[j].astype(jnp.float32)
            squares += t * t
        tacc[...] = squares

    def share(side):
        total = jnp.zeros((2 * KR * E, KC), jnp.float32)
        for g in range(GR):
            inner = acc[g, side]
            high = inner.astype(jnp.bfloat16)
            low = (inner - high.astype(jnp.float32)).astype(jnp.bfloat16)
            total += jnp.dot(spread[g], high, preferred_element_type=jnp.float32)
            total += jnp.dot(spread[g], low, preferred_element_type=jnp.float32)
        part[side] = total.reshape(2, KR * E, KC)

    def exchange():
        share(1)
        for h in range(2):
            push(part.at[1, h], part_in.at[1 + c], ssem.at[7], csem.at[4 + c], at_y(partner_y(c), h))
        share(0)
        push(part.at[0, 1 - c], part_in.at[0], ssem.at[7], msem.at[3], sib)

    prepared = False
    for kind, i, dx, dz, way in SCHEDULE:
        if kind >= 12 and not prepared:
            prepare()
            prepared = True
        if kind == 12 and i == 0:
            share_candidates()
            await_bytes(cot.at[c], lsem.at[4])
            candidate_grads(c)
        elif kind == 12 and i == 1:
            await_bytes(masked.at[1 - c], msem.at[7])
            await_bytes(cot.at[1 - c], csem.at[0])
            candidate_grads(1 - c)
        elif kind == 12:
            for h in range(2):
                await_bytes(masked.at[2 + h], msem.at[1 + h])
                await_bytes(cot.at[2 + h], csem.at[2 + h])
                candidate_grads(2 + h)
        elif kind == 13:
            multiply(i, 0)
        elif kind == 14:
            multiply(i, 1)
        elif kind == 15:
            targets_done(i)
        elif kind == 16:
            exchange()
        else:
            send(kind, i, dx, dz, way)

    tsq[...] = lax.dot_general(
        jnp.ones((2 * E, KC), jnp.float32), tacc[...], (((1,), (1,)), ((), ())),
        precision=lax.Precision.HIGHEST, preferred_element_type=jnp.float32,
    )
    push(tsq, tsq_in, ssem.at[10], msem.at[6], sib)
    await_bytes(tgt_in, msem.at[4])
    await_bytes(tsq_in, msem.at[6])
    await_bytes(part_in.at[0], msem.at[3])
    for h in range(2):
        await_bytes(part_in.at[1 + h], csem.at[4 + h])

    dots = [[jnp.zeros((4 * E, HALF), jnp.float32) for _ in range(2)] for _ in range(2)]
    squares = jnp.zeros((2 * E, KC), jnp.float32)
    for m in range(KR // 2):
        rows = slice(2 * E * m, 2 * E * (m + 1))
        feat = (part[0, c, rows] + part_in[0, rows]) + (part_in[1, rows] + part_in[2, rows])
        squares += feat * feat
        high = feat.astype(jnp.bfloat16).astype(jnp.float32)
        both = jnp.concatenate([high, feat - high], axis=0).astype(jnp.bfloat16)
        for k in range(2):
            for h, t in enumerate((tgt[2 * m + k], tgt_in[2 * m + k])):
                dots[h][k] += lax.dot_general(both, t, (((1,), (1,)), ((), ())), preferred_element_type=jnp.float32)
    sums = jnp.sum(squares, axis=1, keepdims=True)
    cand_norm = jnp.sqrt(sums[:E] + sums[E:] + EPS)
    scores = []
    for h, t in enumerate((tsq, tsq_in)):
        even, late = dots[h]
        product = (even[:E] + even[2 * E : 3 * E]) + (late[E : 2 * E] + late[3 * E :])
        scores.append(math.sqrt(KR * KC) * product / (cand_norm * jnp.sqrt(t[:E] + EPS)))
    pay[:E] = jnp.where(c == 0, scores[0], scores[1])
    pay[E:] = jnp.where(c == 0, scores[1], scores[0])
    pltpu.make_async_copy(pay, land.at[p], msem.at[5]).start()

    for dx, dz in OFFSETS[:0:-1]:
        push(pay, land.at[p], ssem.at[9], msem.at[5], at(x + dx, z + dz))
    for stream, ref in enumerate((big.at[:, pl.ds(0, ZX_ROWS)], big.at[:, pl.ds(0, XZ_ROWS)], tgt.at[:, pl.ds(0, T_GO)])):

        @pl.loop(0, sent[stream] // 8)
        def _(i):
            await_bytes(ref.at[pl.ds(0, 8)], ssem.at[stream])

        @pl.loop(0, sent[stream] % 8)
        def _(i):
            await_bytes(ref.at[0], ssem.at[stream])

    rest = pl.ds(0, NP - 1)
    await_bytes(tgt.at[rest, pl.ds(0, T_Y)], ssem.at[3])
    await_bytes(tgt.at[0, pl.ds(0, 16 * (YS - 1))], ssem.at[4])

    @pl.when(keeper != c)
    def _():
        await_bytes(tgt.at[0, pl.ds(0, 16)], ssem.at[4])

    await_bytes(masked.at[pl.ds(0, 3)], ssem.at[5])
    await_bytes(cot.at[pl.ds(0, 3)], ssem.at[6])
    await_bytes(tgt_in, ssem.at[8])


    await_bytes(land, msem.at[5])
    for j in range(NP):
        for h in range(2):
            out[E * j : E * (j + 1), HALF * h : HALF * (h + 1)] = land[j, E * h : E * (h + 1)]

    await_bytes(part_in, ssem.at[7])
    await_bytes(land.at[rest], ssem.at[9])
    await_bytes(tsq, ssem.at[10])


def on_device(cotangents, adapter_activations, lengths, column_factors, row_factors, targets):
    anywhere = pl.BlockSpec(memory_space=pl.ANY)
    vmem = pl.BlockSpec(memory_space=pltpu.VMEM)
    bf16, f32 = jnp.bfloat16, jnp.float32
    dma = pltpu.SemaphoreType.DMA
    return pl.pallas_call(
        kernel,
        out_shape=jax.ShapeDtypeStruct((NP * E, 2 * HALF), f32),
        in_specs=[anywhere, anywhere, pl.BlockSpec(memory_space=pltpu.SMEM), anywhere, vmem, anywhere],
        out_specs=vmem,
        scratch_shapes=[
            pltpu.VMEM((4, E, TOK, NB * HALF), bf16),
            pltpu.VMEM((E, TOK, RANK), bf16),
            pltpu.VMEM((4, E, TOK, RANK), bf16),
            pltpu.VMEM((4, E, RANK, TOK), bf16),
            pltpu.VMEM((GR, 4 * E * RS, NB * HALF), bf16),
            pltpu.VMEM((NB, GR * HALF, KC), bf16),
            pltpu.VMEM((NP, HALF, KC), bf16),
            pltpu.VMEM((NP, HALF, KC), bf16),
            pltpu.VMEM((GR, 2, 2 * E * RS, KC), f32),
            pltpu.VMEM((GR, KR * 2 * E, 2 * E * RS), bf16),
            pltpu.VMEM((2, 2, KR * E, KC), f32),
            pltpu.VMEM((3, KR * E, KC), f32),
            pltpu.VMEM((HALF, KC), f32),
            pltpu.VMEM((2 * E, HALF), f32),
            pltpu.VMEM((2 * E, HALF), f32),
            pltpu.VMEM((2 * E, HALF), f32),
            pltpu.VMEM((NP, 2 * E, HALF), f32),
            dma((6,)),
            dma((11,)),
            dma((8,)),
            dma((6,)),
            dma((NP,)),
            dma((NP,)),
            dma((NP,)),
            dma((NP,)),
        ],
        compiler_params=pltpu.CompilerParams(collective_id=0, has_side_effects=True, vmem_limit_bytes=56 * 2**20),
        cost_estimate=pl.CostEstimate(flops=3 * 10**9, bytes_accessed=6 * 2**20, transcendentals=0),
    )(cotangents, adapter_activations, lengths, column_factors, row_factors, targets)


def solution(mesh):
    placed = (
        P(("dp", "proj"), None, None),
        P(("dp", "proj"), None, None),
        P(("dp", "proj")),
        P(None, "proj", None),
        P(),
        P("dp", "proj"),
    )
    return jax.shard_map(on_device, mesh=mesh, in_specs=placed, out_specs=P("dp", None), check_vma=False)
```

```python
import functools
import math

import jax
import jax.numpy as jnp
from jax import lax
from jax.experimental import pallas as pl
from jax.experimental.pallas import tpu as pltpu
from jax.sharding import PartitionSpec as P

MESH = pl.DeviceIdType.MESH
EPS = 1e-06
XS, YS, ZS = 4, 8, 8
NP = XS * ZS
GR, RS, KR, KC = 4, 32, 32, 256
E, TOK, RANK = 4, 64, 128
HALF = 128
NB = NP // 2
ZX_ROWS = 336
XZ_ROWS = GR * HALF - ZX_ROWS
T_GO, T_Y = 80, 48


OFFSETS = sorted(
    [(dx, dz) for dx in (0, 1, -1, 2) for dz in (1, -1, 2, -2, 3, -3, 4, 0)], key=lambda o: abs(o[0]) + abs(o[1])
)
BY_PARITY = [[o for o in OFFSETS if sum(o) % 2 == parity] for parity in range(2)]
GROUP = 4
SCHEDULE = [
    (0, 0, 0, 0, "z-"), (0, 0, 0, 0, "z+"), (1, 1, 0, 0, "x+"), (1, 1, 0, 0, "x-"), (12, 0, 0, 0, ""), (1, 1, 1, 0, "x+"),
    (1, 1, -1, 0, "x-"), (0, 0, 0, 0, "x+"), (2, 0, 0, 0, "z-"), (2, 0, 0, 0, "z+"), (0, 0, 0, -1, "z-"), (0, 0, 0, 1, "z+"),
    (2, 1, 0, 0, "x-"), (0, 0, 0, 1, "x+"), (2, 1, 0, 0, "z-"), (2, 1, 0, 0, "z+"), (1, 1, 0, 0, "z+"), (1, 1, 0, 0, "z-"),
    (0, 0, 0, -1, "x-"), (2, 0, 0, 0, "x+"), (0, 0, 0, 0, "x-"), (2, 1, 0, 0, "x+"), (1, 1, -1, 0, "z-"), (2, 0, 0, 1, "z+"),
    (2, 1, -1, 0, "x-"), (1, 1, 1, 0, "z+"), (2, 1, -1, 0, "z-"), (2, 1, 0, 1, "z+"), (2, 0, 0, 1, "x-"), (2, 0, 0, 2, "x+"),
    (0, 0, 0, 1, "x-"), (2, 0, 0, 2, "z+"), (2, 0, 0, -1, "x+"), (2, 0, 0, -2, "x+"), (2, 0, 0, 2, "x-"), (2, 0, 1, -1, "x+"),
    (2, 0, 1, 1, "x+"), (2, 1, 0, -1, "z-"), (2, 0, 0, -1, "z-"), (2, 0, 0, -2, "z-"), (1, 1, 2, 0, "z+"), (1, 1, 2, 0, "z-"),
    (2, 1, 1, 0, "z-"), (2, 0, 0, 1, "x+"), (2, 0, 0, -1, "x-"), (0, 0, 0, -2, "z-"), (0, 0, 0, 2, "z+"), (0, 0, 0, -2, "x+"),
    (0, 0, 0, 2, "x-"), (1, 1, -1, -1, "z-"), (0, 0, 0, -2, "x-"), (0, 0, 0, 2, "x+"), (1, 1, 1, 1, "z+"), (2, 1, 1, 0, "z+"),
    (1, 1, 1, 0, "z-"), (2, 1, 1, 0, "x+"), (2, 0, 0, -2, "x-"), (2, 1, -1, 0, "z+"), (2, 0, 0, -3, "z-"), (2, 1, 2, 0, "z-"),
    (2, 0, -1, 1, "x-"), (1, 1, -1, 0, "z+"), (2, 0, 0, 3, "x+"), (0, 0, 0, -1, "x+"), (2, 0, 0, -3, "x-"), (2, 1, 0, 2, "z+"),
    (1, 1, 0, -1, "z-"), (2, 1, 2, 0, "z+"), (1, 1, 2, 1, "z+"), (2, 0, 0, 3, "z+"), (2, 0, 0, 1, "y"), (2, 1, -1, -1, "z-"),
    (2, 0, -1, -1, "x-"), (2, 1, 1, 1, "z+"), (12, 1, 0, 0, ""), (2, 0, 0, 0, "x-"), (2, 0, 0, 3, "x-"), (2, 1, 1, -1, "z-"),
    (0, 0, 0, -3, "x+"), (2, 0, 1, -2, "x+"), (0, 0, 0, -3, "z-"), (0, 0, 0, 3, "x+"), (0, 0, 0, -3, "x-"), (0, 0, 0, 3, "z+"),
    (0, 0, 0, 3, "x-"), (2, 0, 0, -3, "x+"), (2, 0, 1, 0, "y"), (1, 1, 0, 1, "z+"), (1, 1, 2, -1, "z-"), (2, 0, 2, -1, "y"),
    (2, 1, 1, -2, "z-"), (2, 0, 1, -2, "y"), (2, 0, 0, -1, "y"), (2, 0, 1, 3, "x+"), (2, 1, 0, -2, "z-"), (0, 0, -1, 1, "x-"),
    (2, 1, -1, 1, "z+"), (2, 1, 1, 2, "z+"), (1, 1, -1, 1, "z+"), (2, 0, -1, 0, "y"), (0, 0, -1, -1, "x-"), (2, 1, 2, -1, "z-"),
    (2, 0, 0, 4, "x+"), (0, 0, 1, 1, "x+"), (2, 0, -1, 2, "x-"), (0, 0, 1, -2, "x+"), (1, 1, 1, -1, "z-"), (2, 0, -1, -2, "y"),
    (0, 0, -1, -2, "x-"), (0, 0, 1, -1, "x+"), (2, 1, 2, 1, "z+"), (1, 1, 0, -2, "z-"), (2, 0, 1, -1, "y"), (1, 1, 2, 2, "z+"),
    (2, 0, -1, -1, "y"), (2, 0, -1, -3, "x-"), (2, 0, 1, 2, "x+"), (2, 0, -1, -2, "x-"), (2, 1, -1, 2, "z+"), (0, 0, 0, 4, "x-"),
    (0, 0, 0, 4, "x+"), (2, 0, 1, 0, "x+"), (0, 0, -1, -3, "x-"), (2, 0, 2, 1, "y"), (1, 1, 2, -2, "z-"), (2, 1, -1, -2, "z-"),
    (1, 1, 0, 2, "z+"), (2, 1, 1, 3, "z+"), (2, 0, -1, 3, "x-"), (13, 0, 0, 0, ""), (2, 0, 1, 3, "y"), (0, 0, -1, 3, "x-"),
    (0, 0, 1, 0, "x+"), (2, 0, 0, 3, "y"), (2, 0, 1, -3, "y"), (2, 1, 1, -3, "z-"), (2, 0, 1, -3, "x+"), (1, 1, 1, 2, "z+"),
    (0, 0, 1, 3, "x+"), (2, 1, 2, 2, "z+"), (0, 0, 1, 2, "x+"), (1, 1, 1, -2, "z-"), (2, 0, -1, 2, "y"), (2, 0, 1, 1, "y"),
    (2, 1, 2, -2, "z-"), (2, 0, 0, 2, "y"), (2, 0, 0, 4, "x-"), (0, 0, -1, 2, "x-"), (1, 1, -1, -2, "z-"), (0, 0, -1, 0, "x-"),
    (1, 1, -1, 2, "z+"), (1, 1, 0, -3, "z-"), (1, 1, 2, 3, "z+"), (2, 1, 0, -3, "z-"), (2, 1, -1, -3, "z-"), (0, 0, 1, -3, "x+"),
    (2, 1, -1, 3, "z+"), (12, 2, 0, 0, ""), (1, 1, 1, 3, "z+"), (2, 0, -1, 0, "x-"), (1, 1, 0, 3, "z+"), (0, 0, 1, 4, "x+"),
    (2, 0, -1, 3, "y"), (2, 0, -1, 1, "y"), (0, 0, -1, 4, "x-"), (2, 0, -1, 4, "x-"), (2, 1, 2, 3, "z+"), (1, 1, -1, -3, "z-"),
    (1, 1, 1, -3, "z-"), (2, 0, 1, 2, "y"), (2, 0, 0, -2, "y"), (2, 0, 2, 2, "y"), (1, 1, -1, 3, "z+"), (2, 0, 1, 4, "x+"),
    (1, 1, 2, -3, "z-"), (13, 1, 0, 0, ""), (2, 0, 0, -3, "y"), (2, 0, 2, -2, "y"), (2, 0, 2, -3, "y"), (2, 1, 0, 3, "z+"),
    (14, 1, 0, 0, ""), (2, 0, -1, 4, "y"), (2, 1, 2, -3, "z-"), (14, 0, 0, 0, ""), (2, 0, 2, 3, "y"), (2, 0, -1, -3, "y"),
    (2, 0, 1, 4, "y"), (14, 2, 0, 0, ""), (13, 2, 0, 0, ""), (2, 0, 0, 4, "y"), (2, 0, 2, 0, "y"), (2, 0, 2, 4, "y"),
    (14, 3, 0, 0, ""), (13, 3, 0, 0, ""), (16, 0, 0, 0, ""), (15, 2, 0, 0, ""), (15, 0, 0, 0, ""), (15, 1, 0, 0, ""),
    (15, 3, 0, 0, ""),
]


def kernel(
    cot_hbm, act_hbm, lens, cf_hbm, rf, tg_hbm, out,
    cot, act, masked, flipped, grads, big, tgt, tgt_in, acc, spread, part, part_in, tacc, tsq, tsq_in, pay, land,
    lsem, ssem, msem, csem, rzx, rxz, rt, rty,
):
    a, p = lax.axis_index("dp"), lax.axis_index("proj")
    y, c = a // 2, a % 2
    x, z = p // ZS, p % ZS
    odd = y % 2
    outside = (x + z + odd) % 2
    sib = (y * 2 + 1 - c, p)

    def at(ax, az):
        return (a, ((ax + XS) % XS) * ZS + (az + ZS) % ZS)

    def at_y(ay, core):
        return (((ay + YS) % YS) * 2 + core, p)

    def partner_y(core):
        return y + (1 - 2 * odd) * (1 - 2 * core)

    def push(src, dst, s, r, to):
        pltpu.make_async_remote_copy(src_ref=src, dst_ref=dst, send_sem=s, recv_sem=r, device_id=to, device_id_type=MESH).start()

    def await_bytes(ref, sem):
        pltpu.make_async_copy(ref, ref, sem).wait()

    def cot_columns(q, parity, half):
        sx = q // 4
        j = sx * ZS + 2 * (q % 4) + (sx + parity) % 2
        return cot_hbm.at[:, :, pl.ds(pl.multiple_of(j * 256 + half * HALF, HALF), HALF)]

    def cot_slot(who, q):
        return cot.at[who, :, :, pl.ds(pl.multiple_of(q * HALF, HALF), HALF)]

    own = []
    for g in range(GR):
        own.append(
            pltpu.make_async_copy(
                cf_hbm.at[g, pl.ds(pl.multiple_of(c * HALF, HALF), HALF)], big.at[p // 2, pl.ds(g * HALF, HALF)], lsem.at[g]
            )
        )
    own_act = pltpu.make_async_copy(act_hbm, act, lsem.at[5])

    @pl.when(outside == 0)
    def _():
        for copy in own:
            copy.start()

    bar = pltpu.get_barrier_semaphore()

    greeted = [at(x, z + 1), at(x, z - 1), at(x + 1, z), at(x - 1, z)] + [((a + i) % (2 * YS), p) for i in range(1, 2 * YS)]
    for to in greeted:
        pl.semaphore_signal(bar, inc=1, device_id=to, device_id_type=MESH)

    own_act.start()

    @pl.when(outside == 0)
    def _():
        for copy in own:
            copy.wait()

    pl.semaphore_wait(bar, len(greeted))

    keeper = a // YS
    slot = tgt.at[p, pl.ds(pl.multiple_of(16 * (a % YS), 16), 16)]

    @pl.when(keeper == c)
    def _():
        pltpu.make_async_copy(tg_hbm, slot, msem.at[0]).start()

    @pl.when(keeper != c)
    def _():
        push(tg_hbm, slot, ssem.at[4], msem.at[0], sib)

    @pl.loop(1, YS)
    def _(i):
        push(tg_hbm, slot, ssem.at[4], msem.at[0], at_y(y + i, keeper))

    def zx(j):
        return big.at[j // 2, pl.ds(0, ZX_ROWS)]

    def xz(j):
        return big.at[j // 2, pl.ds(ZX_ROWS, XZ_ROWS)]

    def t_go(j):
        return tgt.at[j, pl.ds(pl.multiple_of(T_Y * odd, 16), T_GO)]

    def t_y(j, plane):
        return tgt.at[j, pl.ds(pl.multiple_of(T_GO * plane, 16), T_Y)]

    PARTS = ((zx, rzx), (xz, rxz), (t_go, rt))

    def source(dx, dz):
        sx, sz = (x - dx + XS) % XS, (z - dz + ZS) % ZS
        return sx, sz, sx * ZS + sz

    def share_candidates():
        @pl.loop(0, NB)
        def _(q):
            pltpu.make_async_copy(cot_columns(q, odd, c), cot_slot(c, q), lsem.at[4]).start()

        own_act.wait()
        tokens = lax.broadcasted_iota(jnp.int32, (TOK, RANK), 0)
        for e in range(E):
            kept = jnp.where(tokens < lens[e], act[e].astype(jnp.float32), 0.0)
            masked[c, e] = kept.astype(jnp.bfloat16)
        for h in range(2):
            push(masked.at[c], masked.at[2 + c], ssem.at[5], msem.at[1 + c], at_y(partner_y(h), h))

        @pl.loop(0, NB)
        def _(q):
            for h in range(2):
                push(cot_columns(q, 1 - odd, h), cot_slot(2 + c, q), ssem.at[6], csem.at[2 + c], at_y(partner_y(h), h))

        push(masked.at[c], masked.at[c], ssem.at[5], msem.at[7], sib)

        @pl.loop(0, NB)
        def _(q):
            push(cot_columns(q, odd, 1 - c), cot_slot(c, q), ssem.at[6], csem.at[0], sib)

    def candidate_grads(who):
        for e in range(E):
            flipped[who, e] = masked[who, e].astype(jnp.float32).T.astype(jnp.bfloat16)

        @pl.loop(0, E)
        def _(e):
            row = pl.ds(pl.multiple_of((who * E + e) * RS, RS), RS)
            g_all = jnp.dot(flipped[who, e], cot[who, e], preferred_element_type=jnp.float32).astype(jnp.bfloat16)
            for g in range(GR):
                grads[g, row, :] = g_all[g * RS : (g + 1) * RS]

    def prepare():
        acc[...] = jnp.zeros_like(acc)
        tacc[...] = jnp.zeros_like(tacc)
        by_row = lax.broadcasted_iota(jnp.int32, (2 * KR * E, KR), 0) % (KR * E) // E
        pick_k = (by_row == lax.broadcasted_iota(jnp.int32, (2 * KR * E, KR), 1)).astype(jnp.bfloat16)
        by_col = lax.broadcasted_iota(jnp.int32, (RS, 2 * E * RS), 1) % RS
        pick_a = (by_col == lax.broadcasted_iota(jnp.int32, (RS, 2 * E * RS), 0)).astype(jnp.bfloat16)
        row = lax.broadcasted_iota(jnp.int32, (256, 256), 0)
        col = lax.broadcasted_iota(jnp.int32, (256, 256), 1) // RS
        same = row // (KR * E) * E + row % E == col
        for g in range(GR):
            by_k = lax.dot_general(pick_k, rf[g], (((1,), (1,)), ((), ())), preferred_element_type=jnp.float32)
            wide = jnp.dot(by_k.astype(jnp.bfloat16), pick_a, preferred_element_type=jnp.float32)
            spread[g] = jnp.where(same, wide, 0.0).astype(jnp.bfloat16)

    held = set()
    sent = [jnp.int32(0)] * 3

    def await_part(stream, dx, dz, parities):
        new = [r for r in parities if (stream, dx, dz, r) not in held]
        held.update((stream, dx, dz, r) for r in new)
        if not new or (dx, dz) == (0, 0) and stream < 2:
            return
        view, sems = PARTS[stream]
        j = source(dx, dz)[2]

        def go():
            if (dx, dz) == (0, 0):
                await_bytes(tgt.at[p], msem.at[0])
            else:
                await_bytes(view(j), sems.at[j])

        if len(new) == 2:
            go()
        else:
            pl.when((dx + dz + outside) % 2 == new[0])(go)

    def send(stream, tree, dx, dz, way):
        sx, sz, j = source(dx, dz)
        view, sems = PARTS[stream]
        if way == "y":
            await_part(stream, dx, dz, (0, 1))
            to_y = 1 - 2 * ((sx + sz // 2) % 2)
            push(t_y(j, odd), t_y(j, odd), ssem.at[3], rty.at[j], at_y(y + to_y, c))
            return
        parity = 0 if stream < 2 else 1 - tree
        await_part(stream, dx, dz, (parity,))
        step = 1 if way[1] == "+" else -1
        to = at(x + step, z) if way[0] == "x" else at(x, z + step)
        applies = (dx + dz + outside) % 2 == parity
        side = (sz if tree == 0 else sx) // 2 % 2
        if way[0] == "z" and abs(dz) == 3:
            applies &= side == (0 if dz > 0 else 1)
        elif way[0] == "x" and abs(dx) == 1:
            applies &= side == (0 if dx > 0 else 1)
        sent[stream] += applies.astype(jnp.int32)

        @pl.when(applies)
        def _():
            push(view(j), view(j), ssem.at[stream], sems.at[j], to)

    def multiply(q, side):
        members = [[offsets[GROUP * q + i] for offsets in BY_PARITY] for i in range(GROUP)]
        for pair in members:
            for o in pair:
                for stream in range(2):
                    await_part(stream, *o, (0,))
        js = [jnp.where(outside == 0, source(*even)[2], source(*odds)[2]) // 2 for even, odds in members]
        rows = slice(256 * side, 256 * (side + 1))
        for g in range(GR):
            left = jnp.concatenate([grads[g, rows, pl.ds(pl.multiple_of(j * HALF, HALF), HALF)] for j in js], axis=1)
            right = jnp.concatenate([big[j, g * HALF : (g + 1) * HALF, :] for j in js], axis=0)
            acc[g, side] += jnp.dot(left, right, preferred_element_type=jnp.float32)

    def targets_done(q):
        js = []
        for dx, dz in OFFSETS[8 * q : 8 * (q + 1)]:
            j = source(dx, dz)[2]
            await_part(2, dx, dz, (0, 1))
            if (dx, dz) != (0, 0):
                await_bytes(t_y(j, 1 - odd), rty.at[j])
            push(tgt.at[j], tgt_in.at[j], ssem.at[8], msem.at[4], sib)
            js.append(j)
        squares = tacc[...]
        for j in js:
            t = tgt[j].astype(jnp.float32)
            squares += t * t
        tacc[...] = squares

    def share(side):
        total = jnp.zeros((2 * KR * E, KC), jnp.float32)
        for g in range(GR):
            inner = acc[g, side]
            high = inner.astype(jnp.bfloat16)
            low = (inner - high.astype(jnp.float32)).astype(jnp.bfloat16)
            total += jnp.dot(spread[g], high, preferred_element_type=jnp.float32)
            total += jnp.dot(spread[g], low, preferred_element_type=jnp.float32)
        part[side] = total.reshape(2, KR * E, KC)

    def exchange():
        share(1)
        for h in range(2):
            push(part.at[1, h], part_in.at[1 + c], ssem.at[7], csem.at[4 + c], at_y(partner_y(c), h))
        share(0)
        push(part.at[0, 1 - c], part_in.at[0], ssem.at[7], msem.at[3], sib)

    prepared = False
    for kind, i, dx, dz, way in SCHEDULE:
        if kind >= 12 and not prepared:
            prepare()
            prepared = True
        if kind == 12 and i == 0:
            share_candidates()
            await_bytes(cot.at[c], lsem.at[4])
            candidate_grads(c)
        elif kind == 12 and i == 1:
            await_bytes(masked.at[1 - c], msem.at[7])
            await_bytes(cot.at[1 - c], csem.at[0])
            candidate_grads(1 - c)
        elif kind == 12:
            for h in range(2):
                await_bytes(masked.at[2 + h], msem.at[1 + h])
                await_bytes(cot.at[2 + h], csem.at[2 + h])
                candidate_grads(2 + h)
        elif kind == 13:
            multiply(i, 0)
        elif kind == 14:
            multiply(i, 1)
        elif kind == 15:
            targets_done(i)
        elif kind == 16:
            exchange()
        else:
            send(kind, i, dx, dz, way)

    tsq[...] = lax.dot_general(
        jnp.ones((2 * E, KC), jnp.float32), tacc[...], (((1,), (1,)), ((), ())),
        precision=lax.Precision.HIGHEST, preferred_element_type=jnp.float32,
    )
    push(tsq, tsq_in, ssem.at[10], msem.at[6], sib)
    await_bytes(tgt_in, msem.at[4])
    await_bytes(tsq_in, msem.at[6])
    await_bytes(part_in.at[0], msem.at[3])
    for h in range(2):
        await_bytes(part_in.at[1 + h], csem.at[4 + h])

    dots = [[jnp.zeros((4 * E, HALF), jnp.float32) for _ in range(2)] for _ in range(2)]
    squares = jnp.zeros((2 * E, KC), jnp.float32)
    for m in range(KR // 2):
        rows = slice(2 * E * m, 2 * E * (m + 1))
        feat = (part[0, c, rows] + part_in[0, rows]) + (part_in[1, rows] + part_in[2, rows])
        squares += feat * feat
        high = feat.astype(jnp.bfloat16).astype(jnp.float32)
        both = jnp.concatenate([high, feat - high], axis=0).astype(jnp.bfloat16)
        for k in range(2):
            for h, t in enumerate((tgt[2 * m + k], tgt_in[2 * m + k])):
                dots[h][k] += lax.dot_general(both, t, (((1,), (1,)), ((), ())), preferred_element_type=jnp.float32)
    sums = jnp.sum(squares, axis=1, keepdims=True)
    cand_norm = jnp.sqrt(sums[:E] + sums[E:] + EPS)
    scores = []
    for h, t in enumerate((tsq, tsq_in)):
        even, late = dots[h]
        product = (even[:E] + even[2 * E : 3 * E]) + (late[E : 2 * E] + late[3 * E :])
        scores.append(math.sqrt(KR * KC) * product / (cand_norm * jnp.sqrt(t[:E] + EPS)))
    pay[:E] = jnp.where(c == 0, scores[0], scores[1])
    pay[E:] = jnp.where(c == 0, scores[1], scores[0])
    pltpu.make_async_copy(pay, land.at[p], msem.at[5]).start()

    for dx, dz in OFFSETS[:0:-1]:
        push(pay, land.at[p], ssem.at[9], msem.at[5], at(x + dx, z + dz))
    for stream, ref in enumerate((big.at[:, pl.ds(0, ZX_ROWS)], big.at[:, pl.ds(0, XZ_ROWS)], tgt.at[:, pl.ds(0, T_GO)])):

        @pl.loop(0, sent[stream] // 8)
        def _(i):
            await_bytes(ref.at[pl.ds(0, 8)], ssem.at[stream])

        @pl.loop(0, sent[stream] % 8)
        def _(i):
            await_bytes(ref.at[0], ssem.at[stream])

    rest = pl.ds(0, NP - 1)
    await_bytes(tgt.at[rest, pl.ds(0, T_Y)], ssem.at[3])
    await_bytes(tgt.at[0, pl.ds(0, 16 * (YS - 1))], ssem.at[4])

    @pl.when(keeper != c)
    def _():
        await_bytes(tgt.at[0, pl.ds(0, 16)], ssem.at[4])

    await_bytes(masked.at[pl.ds(0, 3)], ssem.at[5])
    await_bytes(cot.at[pl.ds(0, 3)], ssem.at[6])
    await_bytes(tgt_in, ssem.at[8])


    await_bytes(land, msem.at[5])
    for j in range(NP):
        for h in range(2):
            out[E * j : E * (j + 1), HALF * h : HALF * (h + 1)] = land[j, E * h : E * (h + 1)]

    await_bytes(part_in, ssem.at[7])
    await_bytes(land.at[rest], ssem.at[9])
    await_bytes(tsq, ssem.at[10])


def on_device(cotangents, adapter_activations, lengths, column_factors, row_factors, targets):
    anywhere = pl.BlockSpec(memory_space=pl.ANY)
    vmem = pl.BlockSpec(memory_space=pltpu.VMEM)
    bf16, f32 = jnp.bfloat16, jnp.float32
    dma = pltpu.SemaphoreType.DMA
    return pl.pallas_call(
        kernel,
        out_shape=jax.ShapeDtypeStruct((NP * E, 2 * HALF), f32),
        in_specs=[anywhere, anywhere, pl.BlockSpec(memory_space=pltpu.SMEM), anywhere, vmem, anywhere],
        out_specs=vmem,
        scratch_shapes=[
            pltpu.VMEM((4, E, TOK, NB * HALF), bf16),
            pltpu.VMEM((E, TOK, RANK), bf16),
            pltpu.VMEM((4, E, TOK, RANK), bf16),
            pltpu.VMEM((4, E, RANK, TOK), bf16),
            pltpu.VMEM((GR, 4 * E * RS, NB * HALF), bf16),
            pltpu.VMEM((NB, GR * HALF, KC), bf16),
            pltpu.VMEM((NP, HALF, KC), bf16),
            pltpu.VMEM((NP, HALF, KC), bf16),
            pltpu.VMEM((GR, 2, 2 * E * RS, KC), f32),
            pltpu.VMEM((GR, KR * 2 * E, 2 * E * RS), bf16),
            pltpu.VMEM((2, 2, KR * E, KC), f32),
            pltpu.VMEM((3, KR * E, KC), f32),
            pltpu.VMEM((HALF, KC), f32),
            pltpu.VMEM((2 * E, HALF), f32),
            pltpu.VMEM((2 * E, HALF), f32),
            pltpu.VMEM((2 * E, HALF), f32),
            pltpu.VMEM((NP, 2 * E, HALF), f32),
            dma((6,)),
            dma((11,)),
            dma((8,)),
            dma((6,)),
            dma((NP,)),
            dma((NP,)),
            dma((NP,)),
            dma((NP,)),
        ],
        compiler_params=pltpu.CompilerParams(collective_id=0, has_side_effects=True, vmem_limit_bytes=56 * 2**20),
        cost_estimate=pl.CostEstimate(flops=3 * 10**9, bytes_accessed=6 * 2**20, transcendentals=0),
    )(cotangents, adapter_activations, lengths, column_factors, row_factors, targets)


def solution(mesh):
    placed = (
        P(("dp", "proj"), None, None),
        P(("dp", "proj"), None, None),
        P(("dp", "proj")),
        P(None, "proj", None),
        P(),
        P("dp", "proj"),
    )
    return jax.shard_map(on_device, mesh=mesh, in_specs=placed, out_specs=P("dp", None), check_vma=False)
```

```python
import functools
import math

import jax
import jax.numpy as jnp
from jax import lax
from jax.experimental import pallas as pl
from jax.experimental.pallas import tpu as pltpu
from jax.sharding import PartitionSpec as P

MESH = pl.DeviceIdType.MESH
EPS = 1e-06
XS, YS, ZS = 4, 8, 8
NP = XS * ZS
GR, RS, KR, KC = 4, 32, 32, 256
E, TOK, RANK = 4, 64, 128
HALF = 128
NB = NP // 2
ZX_ROWS = 336
XZ_ROWS = GR * HALF - ZX_ROWS
T_GO, T_Y = 80, 48


OFFSETS = sorted(
    [(dx, dz) for dx in (0, 1, -1, 2) for dz in (1, -1, 2, -2, 3, -3, 4, 0)], key=lambda o: abs(o[0]) + abs(o[1])
)
BY_PARITY = [[o for o in OFFSETS if sum(o) % 2 == parity] for parity in range(2)]
GROUP = 4
SCHEDULE = [
    (0, 0, 0, 0, "z-"), (0, 0, 0, 0, "z+"), (1, 1, 0, 0, "x+"), (1, 1, 0, 0, "x-"), (12, 0, 0, 0, ""), (1, 1, 1, 0, "x+"),
    (1, 1, -1, 0, "x-"), (0, 0, 0, 0, "x+"), (2, 0, 0, 0, "z-"), (2, 0, 0, 0, "z+"), (0, 0, 0, -1, "z-"), (0, 0, 0, 1, "z+"),
    (2, 1, 0, 0, "x-"), (0, 0, 0, 1, "x+"), (2, 1, 0, 0, "z-"), (2, 1, 0, 0, "z+"), (1, 1, 0, 0, "z+"), (1, 1, 0, 0, "z-"),
    (0, 0, 0, -1, "x-"), (2, 0, 0, 0, "x+"), (0, 0, 0, 0, "x-"), (2, 1, 0, 0, "x+"), (1, 1, -1, 0, "z-"), (2, 0, 0, 1, "z+"),
    (2, 1, -1, 0, "x-"), (1, 1, 1, 0, "z+"), (2, 1, -1, 0, "z-"), (2, 1, 0, 1, "z+"), (2, 0, 0, 1, "x-"), (2, 0, 0, 2, "x+"),
    (0, 0, 0, 1, "x-"), (2, 0, 0, 2, "z+"), (2, 0, 0, -1, "x+"), (2, 0, 0, -2, "x+"), (2, 0, 0, 2, "x-"), (2, 0, 1, -1, "x+"),
    (2, 0, 1, 1, "x+"), (2, 1, 0, -1, "z-"), (2, 0, 0, -1, "z-"), (2, 0, 0, -2, "z-"), (1, 1, 2, 0, "z+"), (1, 1, 2, 0, "z-"),
    (2, 1, 1, 0, "z-"), (2, 0, 0, 1, "x+"), (2, 0, 0, -1, "x-"), (0, 0, 0, -2, "z-"), (0, 0, 0, 2, "z+"), (0, 0, 0, -2, "x+"),
    (0, 0, 0, 2, "x-"), (1, 1, -1, -1, "z-"), (0, 0, 0, -2, "x-"), (0, 0, 0, 2, "x+"), (1, 1, 1, 1, "z+"), (2, 1, 1, 0, "z+"),
    (1, 1, 1, 0, "z-"), (2, 1, 1, 0, "x+"), (2, 0, 0, -2, "x-"), (2, 1, -1, 0, "z+"), (2, 0, 0, -3, "z-"), (2, 1, 2, 0, "z-"),
    (2, 0, -1, 1, "x-"), (1, 1, -1, 0, "z+"), (2, 0, 0, 3, "x+"), (0, 0, 0, -1, "x+"), (2, 0, 0, -3, "x-"), (2, 1, 0, 2, "z+"),
    (1, 1, 0, -1, "z-"), (2, 1, 2, 0, "z+"), (1, 1, 2, 1, "z+"), (2, 0, 0, 3, "z+"), (2, 0, 0, 1, "y"), (2, 1, -1, -1, "z-"),
    (2, 0, -1, -1, "x-"), (2, 1, 1, 1, "z+"), (12, 1, 0, 0, ""), (2, 0, 0, 0, "x-"), (2, 0, 0, 3, "x-"), (2, 1, 1, -1, "z-"),
    (0, 0, 0, -3, "x+"), (2, 0, 1, -2, "x+"), (0, 0, 0, -3, "z-"), (0, 0, 0, 3, "x+"), (0, 0, 0, -3, "x-"), (0, 0, 0, 3, "z+"),
    (0, 0, 0, 3, "x-"), (2, 0, 0, -3, "x+"), (2, 0, 1, 0, "y"), (1, 1, 0, 1, "z+"), (1, 1, 2, -1, "z-"), (2, 0, 2, -1, "y"),
    (2, 1, 1, -2, "z-"), (2, 0, 1, -2, "y"), (2, 0, 0, -1, "y"), (2, 0, 1, 3, "x+"), (2, 1, 0, -2, "z-"), (0, 0, -1, 1, "x-"),
    (2, 1, -1, 1, "z+"), (2, 1, 1, 2, "z+"), (1, 1, -1, 1, "z+"), (2, 0, -1, 0, "y"), (0, 0, -1, -1, "x-"), (2, 1, 2, -1, "z-"),
    (2, 0, 0, 4, "x+"), (0, 0, 1, 1, "x+"), (2, 0, -1, 2, "x-"), (0, 0, 1, -2, "x+"), (1, 1, 1, -1, "z-"), (2, 0, -1, -2, "y"),
    (0, 0, -1, -2, "x-"), (0, 0, 1, -1, "x+"), (2, 1, 2, 1, "z+"), (1, 1, 0, -2, "z-"), (2, 0, 1, -1, "y"), (1, 1, 2, 2, "z+"),
    (2, 0, -1, -1, "y"), (2, 0, -1, -3, "x-"), (2, 0, 1, 2, "x+"), (2, 0, -1, -2, "x-"), (2, 1, -1, 2, "z+"), (0, 0, 0, 4, "x-"),
    (0, 0, 0, 4, "x+"), (2, 0, 1, 0, "x+"), (0, 0, -1, -3, "x-"), (2, 0, 2, 1, "y"), (1, 1, 2, -2, "z-"), (2, 1, -1, -2, "z-"),
    (1, 1, 0, 2, "z+"), (2, 1, 1, 3, "z+"), (2, 0, -1, 3, "x-"), (13, 0, 0, 0, ""), (2, 0, 1, 3, "y"), (0, 0, -1, 3, "x-"),
    (0, 0, 1, 0, "x+"), (2, 0, 0, 3, "y"), (2, 0, 1, -3, "y"), (2, 1, 1, -3, "z-"), (2, 0, 1, -3, "x+"), (1, 1, 1, 2, "z+"),
    (0, 0, 1, 3, "x+"), (2, 1, 2, 2, "z+"), (0, 0, 1, 2, "x+"), (1, 1, 1, -2, "z-"), (2, 0, -1, 2, "y"), (2, 0, 1, 1, "y"),
    (2, 1, 2, -2, "z-"), (2, 0, 0, 2, "y"), (2, 0, 0, 4, "x-"), (0, 0, -1, 2, "x-"), (1, 1, -1, -2, "z-"), (0, 0, -1, 0, "x-"),
    (1, 1, -1, 2, "z+"), (1, 1, 0, -3, "z-"), (1, 1, 2, 3, "z+"), (2, 1, 0, -3, "z-"), (2, 1, -1, -3, "z-"), (0, 0, 1, -3, "x+"),
    (2, 1, -1, 3, "z+"), (12, 2, 0, 0, ""), (1, 1, 1, 3, "z+"), (2, 0, -1, 0, "x-"), (1, 1, 0, 3, "z+"), (0, 0, 1, 4, "x+"),
    (2, 0, -1, 3, "y"), (2, 0, -1, 1, "y"), (0, 0, -1, 4, "x-"), (2, 0, -1, 4, "x-"), (2, 1, 2, 3, "z+"), (1, 1, -1, -3, "z-"),
    (1, 1, 1, -3, "z-"), (2, 0, 1, 2, "y"), (2, 0, 0, -2, "y"), (2, 0, 2, 2, "y"), (1, 1, -1, 3, "z+"), (2, 0, 1, 4, "x+"),
    (1, 1, 2, -3, "z-"), (13, 1, 0, 0, ""), (2, 0, 0, -3, "y"), (2, 0, 2, -2, "y"), (2, 0, 2, -3, "y"), (2, 1, 0, 3, "z+"),
    (14, 1, 0, 0, ""), (2, 0, -1, 4, "y"), (2, 1, 2, -3, "z-"), (14, 0, 0, 0, ""), (2, 0, 2, 3, "y"), (2, 0, -1, -3, "y"),
    (2, 0, 1, 4, "y"), (14, 2, 0, 0, ""), (13, 2, 0, 0, ""), (2, 0, 0, 4, "y"), (2, 0, 2, 0, "y"), (2, 0, 2, 4, "y"),
    (14, 3, 0, 0, ""), (13, 3, 0, 0, ""), (16, 0, 0, 0, ""), (15, 2, 0, 0, ""), (15, 0, 0, 0, ""), (15, 1, 0, 0, ""),
    (15, 3, 0, 0, ""),
]


def kernel(
    cot_hbm, act_hbm, lens, cf_hbm, rf, tg_hbm, land,
    cot, act, masked, flipped, grads, big, tgt, tgt_in, acc, spread, part, part_in, tacc, tsq, tsq_in, pay,
    lsem, ssem, msem, csem, rzx, rxz, rt, rty,
):
    a, p = lax.axis_index("dp"), lax.axis_index("proj")
    y, c = a // 2, a % 2
    x, z = p // ZS, p % ZS
    odd = y % 2
    outside = (x + z + odd) % 2
    sib = (y * 2 + 1 - c, p)

    def at(ax, az):
        return (a, ((ax + XS) % XS) * ZS + (az + ZS) % ZS)

    def at_y(ay, core):
        return (((ay + YS) % YS) * 2 + core, p)

    def partner_y(core):
        return y + (1 - 2 * odd) * (1 - 2 * core)

    def push(src, dst, s, r, to):
        pltpu.make_async_remote_copy(src_ref=src, dst_ref=dst, send_sem=s, recv_sem=r, device_id=to, device_id_type=MESH).start()

    def await_bytes(ref, sem):
        pltpu.make_async_copy(ref, ref, sem).wait()

    def cot_columns(q, parity, half):
        sx = q // 4
        j = sx * ZS + 2 * (q % 4) + (sx + parity) % 2
        return cot_hbm.at[:, :, pl.ds(pl.multiple_of(j * 256 + half * HALF, HALF), HALF)]

    def cot_slot(who, q):
        return cot.at[who, :, :, pl.ds(pl.multiple_of(q * HALF, HALF), HALF)]

    own = []
    for g in range(GR):
        own.append(
            pltpu.make_async_copy(
                cf_hbm.at[g, pl.ds(pl.multiple_of(c * HALF, HALF), HALF)], big.at[p // 2, pl.ds(g * HALF, HALF)], lsem.at[g]
            )
        )
    own_act = pltpu.make_async_copy(act_hbm, act, lsem.at[5])

    @pl.when(outside == 0)
    def _():
        for copy in own:
            copy.start()

    bar = pltpu.get_barrier_semaphore()

    greeted = [at(x, z + 1), at(x, z - 1), at(x + 1, z), at(x - 1, z)] + [((a + i) % (2 * YS), p) for i in range(1, 2 * YS)]
    for to in greeted:
        pl.semaphore_signal(bar, inc=1, device_id=to, device_id_type=MESH)

    own_act.start()

    @pl.when(outside == 0)
    def _():
        for copy in own:
            copy.wait()

    pl.semaphore_wait(bar, len(greeted))

    keeper = a // YS
    slot = tgt.at[p, pl.ds(pl.multiple_of(16 * (a % YS), 16), 16)]

    @pl.when(keeper == c)
    def _():
        pltpu.make_async_copy(tg_hbm, slot, msem.at[0]).start()

    @pl.when(keeper != c)
    def _():
        push(tg_hbm, slot, ssem.at[4], msem.at[0], sib)

    @pl.loop(1, YS)
    def _(i):
        push(tg_hbm, slot, ssem.at[4], msem.at[0], at_y(y + i, keeper))

    def zx(j):
        return big.at[j // 2, pl.ds(0, ZX_ROWS)]

    def xz(j):
        return big.at[j // 2, pl.ds(ZX_ROWS, XZ_ROWS)]

    def t_go(j):
        return tgt.at[j, pl.ds(pl.multiple_of(T_Y * odd, 16), T_GO)]

    def t_y(j, plane):
        return tgt.at[j, pl.ds(pl.multiple_of(T_GO * plane, 16), T_Y)]

    PARTS = ((zx, rzx), (xz, rxz), (t_go, rt))

    def source(dx, dz):
        sx, sz = (x - dx + XS) % XS, (z - dz + ZS) % ZS
        return sx, sz, sx * ZS + sz

    def share_candidates():
        @pl.loop(0, NB)
        def _(q):
            pltpu.make_async_copy(cot_columns(q, odd, c), cot_slot(c, q), lsem.at[4]).start()

        own_act.wait()
        tokens = lax.broadcasted_iota(jnp.int32, (TOK, RANK), 0)
        for e in range(E):
            kept = jnp.where(tokens < lens[e], act[e].astype(jnp.float32), 0.0)
            masked[c, e] = kept.astype(jnp.bfloat16)
        for h in range(2):
            push(masked.at[c], masked.at[2 + c], ssem.at[5], msem.at[1 + c], at_y(partner_y(h), h))

        @pl.loop(0, NB)
        def _(q):
            for h in range(2):
                push(cot_columns(q, 1 - odd, h), cot_slot(2 + c, q), ssem.at[6], csem.at[2 + c], at_y(partner_y(h), h))

        push(masked.at[c], masked.at[c], ssem.at[5], msem.at[7], sib)

        @pl.loop(0, NB)
        def _(q):
            push(cot_columns(q, odd, 1 - c), cot_slot(c, q), ssem.at[6], csem.at[0], sib)

    def candidate_grads(who):
        for e in range(E):
            flipped[who, e] = masked[who, e].astype(jnp.float32).T.astype(jnp.bfloat16)

        @pl.loop(0, E)
        def _(e):
            row = pl.ds(pl.multiple_of((who * E + e) * RS, RS), RS)
            g_all = jnp.dot(flipped[who, e], cot[who, e], preferred_element_type=jnp.float32).astype(jnp.bfloat16)
            for g in range(GR):
                grads[g, row, :] = g_all[g * RS : (g + 1) * RS]

    def prepare():
        acc[...] = jnp.zeros_like(acc)
        tacc[...] = jnp.zeros_like(tacc)
        by_row = lax.broadcasted_iota(jnp.int32, (2 * KR * E, KR), 0) % (KR * E) // E
        pick_k = (by_row == lax.broadcasted_iota(jnp.int32, (2 * KR * E, KR), 1)).astype(jnp.bfloat16)
        by_col = lax.broadcasted_iota(jnp.int32, (RS, 2 * E * RS), 1) % RS
        pick_a = (by_col == lax.broadcasted_iota(jnp.int32, (RS, 2 * E * RS), 0)).astype(jnp.bfloat16)
        row = lax.broadcasted_iota(jnp.int32, (256, 256), 0)
        col = lax.broadcasted_iota(jnp.int32, (256, 256), 1) // RS
        same = row // (KR * E) * E + row % E == col
        for g in range(GR):
            by_k = lax.dot_general(pick_k, rf[g], (((1,), (1,)), ((), ())), preferred_element_type=jnp.float32)
            wide = jnp.dot(by_k.astype(jnp.bfloat16), pick_a, preferred_element_type=jnp.float32)
            spread[g] = jnp.where(same, wide, 0.0).astype(jnp.bfloat16)

    held = set()
    sent = [jnp.int32(0)] * 3

    def await_part(stream, dx, dz, parities):
        new = [r for r in parities if (stream, dx, dz, r) not in held]
        held.update((stream, dx, dz, r) for r in new)
        if not new or (dx, dz) == (0, 0) and stream < 2:
            return
        view, sems = PARTS[stream]
        j = source(dx, dz)[2]

        def go():
            if (dx, dz) == (0, 0):
                await_bytes(tgt.at[p], msem.at[0])
            else:
                await_bytes(view(j), sems.at[j])

        if len(new) == 2:
            go()
        else:
            pl.when((dx + dz + outside) % 2 == new[0])(go)

    def send(stream, tree, dx, dz, way):
        sx, sz, j = source(dx, dz)
        view, sems = PARTS[stream]
        if way == "y":
            await_part(stream, dx, dz, (0, 1))
            to_y = 1 - 2 * ((sx + sz // 2) % 2)
            push(t_y(j, odd), t_y(j, odd), ssem.at[3], rty.at[j], at_y(y + to_y, c))
            return
        parity = 0 if stream < 2 else 1 - tree
        await_part(stream, dx, dz, (parity,))
        step = 1 if way[1] == "+" else -1
        to = at(x + step, z) if way[0] == "x" else at(x, z + step)
        applies = (dx + dz + outside) % 2 == parity
        side = (sz if tree == 0 else sx) // 2 % 2
        if way[0] == "z" and abs(dz) == 3:
            applies &= side == (0 if dz > 0 else 1)
        elif way[0] == "x" and abs(dx) == 1:
            applies &= side == (0 if dx > 0 else 1)
        sent[stream] += applies.astype(jnp.int32)

        @pl.when(applies)
        def _():
            push(view(j), view(j), ssem.at[stream], sems.at[j], to)

    def multiply(q, side):
        members = [[offsets[GROUP * q + i] for offsets in BY_PARITY] for i in range(GROUP)]
        for pair in members:
            for o in pair:
                for stream in range(2):
                    await_part(stream, *o, (0,))
        js = [jnp.where(outside == 0, source(*even)[2], source(*odds)[2]) // 2 for even, odds in members]
        rows = slice(256 * side, 256 * (side + 1))
        for g in range(GR):
            left = jnp.concatenate([grads[g, rows, pl.ds(pl.multiple_of(j * HALF, HALF), HALF)] for j in js], axis=1)
            right = jnp.concatenate([big[j, g * HALF : (g + 1) * HALF, :] for j in js], axis=0)
            acc[g, side] += jnp.dot(left, right, preferred_element_type=jnp.float32)

    def targets_done(q):
        js = []
        for dx, dz in OFFSETS[8 * q : 8 * (q + 1)]:
            j = source(dx, dz)[2]
            await_part(2, dx, dz, (0, 1))
            if (dx, dz) != (0, 0):
                await_bytes(t_y(j, 1 - odd), rty.at[j])
            push(tgt.at[j], tgt_in.at[j], ssem.at[8], msem.at[4], sib)
            js.append(j)
        squares = tacc[...]
        for j in js:
            t = tgt[j].astype(jnp.float32)
            squares += t * t
        tacc[...] = squares

    def share(side):
        total = jnp.zeros((2 * KR * E, KC), jnp.float32)
        for g in range(GR):
            inner = acc[g, side]
            high = inner.astype(jnp.bfloat16)
            low = (inner - high.astype(jnp.float32)).astype(jnp.bfloat16)
            total += jnp.dot(spread[g], high, preferred_element_type=jnp.float32)
            total += jnp.dot(spread[g], low, preferred_element_type=jnp.float32)
        part[side] = total.reshape(2, KR * E, KC)

    def exchange():
        share(1)
        for h in range(2):
            push(part.at[1, h], part_in.at[1 + c], ssem.at[7], csem.at[4 + c], at_y(partner_y(c), h))
        share(0)
        push(part.at[0, 1 - c], part_in.at[0], ssem.at[7], msem.at[3], sib)

    prepared = False
    for kind, i, dx, dz, way in SCHEDULE:
        if kind >= 12 and not prepared:
            prepare()
            prepared = True
        if kind == 12 and i == 0:
            share_candidates()
            await_bytes(cot.at[c], lsem.at[4])
            candidate_grads(c)
        elif kind == 12 and i == 1:
            await_bytes(masked.at[1 - c], msem.at[7])
            await_bytes(cot.at[1 - c], csem.at[0])
            candidate_grads(1 - c)
        elif kind == 12:
            for h in range(2):
                await_bytes(masked.at[2 + h], msem.at[1 + h])
                await_bytes(cot.at[2 + h], csem.at[2 + h])
                candidate_grads(2 + h)
        elif kind == 13:
            multiply(i, 0)
        elif kind == 14:
            multiply(i, 1)
        elif kind == 15:
            targets_done(i)
        elif kind == 16:
            exchange()
        else:
            send(kind, i, dx, dz, way)

    tsq[...] = lax.dot_general(
        jnp.ones((2 * E, KC), jnp.float32), tacc[...], (((1,), (1,)), ((), ())),
        precision=lax.Precision.HIGHEST, preferred_element_type=jnp.float32,
    )
    push(tsq, tsq_in, ssem.at[10], msem.at[6], sib)
    await_bytes(tgt_in, msem.at[4])
    await_bytes(tsq_in, msem.at[6])
    await_bytes(part_in.at[0], msem.at[3])
    for h in range(2):
        await_bytes(part_in.at[1 + h], csem.at[4 + h])

    dots = [[jnp.zeros((4 * E, HALF), jnp.float32) for _ in range(2)] for _ in range(2)]
    squares = jnp.zeros((2 * E, KC), jnp.float32)
    for m in range(KR // 2):
        rows = slice(2 * E * m, 2 * E * (m + 1))
        feat = (part[0, c, rows] + part_in[0, rows]) + (part_in[1, rows] + part_in[2, rows])
        squares += feat * feat
        high = feat.astype(jnp.bfloat16).astype(jnp.float32)
        both = jnp.concatenate([high, feat - high], axis=0).astype(jnp.bfloat16)
        for k in range(2):
            for h, t in enumerate((tgt[2 * m + k], tgt_in[2 * m + k])):
                dots[h][k] += lax.dot_general(both, t, (((1,), (1,)), ((), ())), preferred_element_type=jnp.float32)
    sums = jnp.sum(squares, axis=1, keepdims=True)
    cand_norm = jnp.sqrt(sums[:E] + sums[E:] + EPS)
    scores = []
    for h, t in enumerate((tsq, tsq_in)):
        even, late = dots[h]
        product = (even[:E] + even[2 * E : 3 * E]) + (late[E : 2 * E] + late[3 * E :])
        scores.append(math.sqrt(KR * KC) * product / (cand_norm * jnp.sqrt(t[:E] + EPS)))
    pay[:E] = jnp.where(c == 0, scores[0], scores[1])
    pay[E:] = jnp.where(c == 0, scores[1], scores[0])
    pltpu.make_async_copy(pay, land.at[p], msem.at[5]).start()

    for dx, dz in OFFSETS[:0:-1]:
        push(pay, land.at[p], ssem.at[9], msem.at[5], at(x + dx, z + dz))
    for stream, ref in enumerate((big.at[:, pl.ds(0, ZX_ROWS)], big.at[:, pl.ds(0, XZ_ROWS)], tgt.at[:, pl.ds(0, T_GO)])):

        @pl.loop(0, sent[stream] // 8)
        def _(i):
            await_bytes(ref.at[pl.ds(0, 8)], ssem.at[stream])

        @pl.loop(0, sent[stream] % 8)
        def _(i):
            await_bytes(ref.at[0], ssem.at[stream])

    rest = pl.ds(0, NP - 1)
    await_bytes(tgt.at[rest, pl.ds(0, T_Y)], ssem.at[3])
    await_bytes(tgt.at[0, pl.ds(0, 16 * (YS - 1))], ssem.at[4])

    @pl.when(keeper != c)
    def _():
        await_bytes(tgt.at[0, pl.ds(0, 16)], ssem.at[4])

    await_bytes(masked.at[pl.ds(0, 3)], ssem.at[5])
    await_bytes(cot.at[pl.ds(0, 3)], ssem.at[6])
    await_bytes(tgt_in, ssem.at[8])


    await_bytes(land, msem.at[5])
    await_bytes(part_in, ssem.at[7])
    await_bytes(land.at[rest], ssem.at[9])
    await_bytes(tsq, ssem.at[10])


def on_device(cotangents, adapter_activations, lengths, column_factors, row_factors, targets):
    anywhere = pl.BlockSpec(memory_space=pl.ANY)
    vmem = pl.BlockSpec(memory_space=pltpu.VMEM)
    bf16, f32 = jnp.bfloat16, jnp.float32
    dma = pltpu.SemaphoreType.DMA
    scores = pl.pallas_call(
        kernel,
        out_shape=jax.ShapeDtypeStruct((NP, 2 * E, HALF), f32),
        in_specs=[anywhere, anywhere, pl.BlockSpec(memory_space=pltpu.SMEM), anywhere, vmem, anywhere],
        out_specs=vmem,
        scratch_shapes=[
            pltpu.VMEM((4, E, TOK, NB * HALF), bf16),
            pltpu.VMEM((E, TOK, RANK), bf16),
            pltpu.VMEM((4, E, TOK, RANK), bf16),
            pltpu.VMEM((4, E, RANK, TOK), bf16),
            pltpu.VMEM((GR, 4 * E * RS, NB * HALF), bf16),
            pltpu.VMEM((NB, GR * HALF, KC), bf16),
            pltpu.VMEM((NP, HALF, KC), bf16),
            pltpu.VMEM((NP, HALF, KC), bf16),
            pltpu.VMEM((GR, 2, 2 * E * RS, KC), f32),
            pltpu.VMEM((GR, KR * 2 * E, 2 * E * RS), bf16),
            pltpu.VMEM((2, 2, KR * E, KC), f32),
            pltpu.VMEM((3, KR * E, KC), f32),
            pltpu.VMEM((HALF, KC), f32),
            pltpu.VMEM((2 * E, HALF), f32),
            pltpu.VMEM((2 * E, HALF), f32),
            pltpu.VMEM((2 * E, HALF), f32),
            dma((6,)),
            dma((11,)),
            dma((8,)),
            dma((6,)),
            dma((NP,)),
            dma((NP,)),
            dma((NP,)),
            dma((NP,)),
        ],
        compiler_params=pltpu.CompilerParams(collective_id=0, has_side_effects=True, vmem_limit_bytes=56 * 2**20),
        cost_estimate=pl.CostEstimate(flops=3 * 10**9, bytes_accessed=6 * 2**20, transcendentals=0),
    )(cotangents, adapter_activations, lengths, column_factors, row_factors, targets)
    return scores.reshape(NP, 2, E, HALF).transpose(0, 2, 1, 3).reshape(NP * E, 2 * HALF)


def solution(mesh):
    placed = (
        P(("dp", "proj"), None, None),
        P(("dp", "proj"), None, None),
        P(("dp", "proj")),
        P(None, "proj", None),
        P(),
        P("dp", "proj"),
    )
    return jax.shard_map(on_device, mesh=mesh, in_specs=placed, out_specs=P("dp", None), check_vma=False)
```
